256 devices in a mesh: row: 8 (over z), col: 16 (over y_hi, x, core), layer: 2 (over y_lo).
Axes of the slice: x: 4, y: 4 (y_hi: 2, y_lo: 2; y = y_hi * 2 + y_lo), z: 8, core: 2. Of those that a mesh axis runs over, the one named last changes fastest.
Arguments:
- x_blocks: bfloat16 [256, 64, 4096], P('row', None, ('col', 'layer')), may hold values from -6 to 6
- x_cols: int32 [256, 64], P('row', ('col', 'layer')), may hold values from 0 to 3, as said below
- x_scales: int32 [256, 64], P('row', ('col', 'layer')), may hold values from 0 to 15
- x_counts: int32 [256, 32], P('row', ('col', 'layer')), may hold values from 0 to 2, as said below
- scale_table: float32 [16], replicated, may hold values from 0.25 to 4
- s_panel: bfloat16 [16, 2, 128, 4096], P('row', 'layer', None, 'col'), may hold values from -0.09375 to 0.09375
- s_rows: int32 [16, 2, 2, 64], P('row', 'layer', None, 'col'), may hold values from 0 to 3, as said below
- s_counts: int32 [16, 2, 64], P('row', 'layer', 'col'), may hold values from 0 to 2, as said below
Outputs:
- product: bfloat16 [16384, 4096], P(('row', 'layer'), 'col')
The draws below stay inside these ranges and needn't reach their ends.
Inputs may be any that keep to these rules, and one draw needn't show every extreme that they name: `x_cols`: within one block row and piece, the 2 slots name different block columns. `x_counts`: in every draw a band of block rows holds 2 live slots in every piece. `s_rows`: within one block column and piece, the 2 slots name different block rows. `s_counts`: in every draw a band of block columns holds 2 live slots in every piece.
All inputs are finite; a program needn't handle non-finite values.
Results may differ from the reference program's by a relative error of at most 0.0049.
Values may be sent and summed in bfloat16 or wider, within the bound.
A program may use at most 64 MiB of HBM per device.

```python
import math
import jax
import jax.numpy as jnp
from jax import lax

BLK = 64
W = 2
KPB = 4
NSCALE = 16
PIECES = 32
NI = 256
NJ = 64
N_COL = 16
N_LAYER = 2


def draw_x_cols(key, part):
    key = jax.random.fold_in(key, 11)
    raw_scores = jax.random.randint(key, (NI, PIECES, KPB), 0, 1 << 20)
    scores = raw_scores * KPB + lax.broadcasted_iota(jnp.int32, (NI, PIECES, KPB), 2)
    chosen = lax.top_k(scores, W)[1]
    return chosen.astype(jnp.int32).reshape(NI, PIECES * W)


def draw_x_counts(key, part):
    key = jax.random.fold_in(key, 23)
    first_key, second_key = jax.random.split(key)
    loose_counts = jax.random.randint(first_key, (NI, PIECES), 0, W + 1)
    band_start = jax.random.randint(second_key, (), 0, NI - NI // 4 + 1)
    row_ids = lax.broadcasted_iota(jnp.int32, (NI, PIECES), 0)
    in_band = (row_ids >= band_start) & (row_ids < band_start + NI // 4)
    return jnp.where(in_band, W, loose_counts).astype(jnp.int32)


def draw_s_rows(key, part):
    key = jax.random.fold_in(key, 37)
    raw_scores = jax.random.randint(key, (PIECES, NJ, KPB), 0, 1 << 20)
    scores = raw_scores * KPB + lax.broadcasted_iota(jnp.int32, (PIECES, NJ, KPB), 2)
    chosen = lax.top_k(scores, W)[1].astype(jnp.int32)
    return jnp.transpose(chosen, (0, 2, 1)).reshape(N_COL, N_LAYER, W, NJ)


def draw_s_counts(key, part):
    key = jax.random.fold_in(key, 41)
    first_key, second_key = jax.random.split(key)
    loose_counts = jax.random.randint(first_key, (PIECES, NJ), 0, W + 1)
    band_start = jax.random.randint(second_key, (), 0, NJ - NJ // 4 + 1)
    col_ids = lax.broadcasted_iota(jnp.int32, (PIECES, NJ), 1)
    in_band = (col_ids >= band_start) & (col_ids < band_start + NJ // 4)
    return jnp.where(in_band, W, loose_counts).astype(jnp.int32).reshape(N_COL, N_LAYER, NJ)


def touch_ends(drawn, stream_key, smallest, top_value):
    shape = drawn.shape
    place = [jax.random.randint(jax.random.fold_in(stream_key, axis), (), 0, shape[axis]) for axis in range(len(shape))]
    drawn = drawn.at[tuple(place)].set(smallest)
    longest = shape.index(max(shape))
    place[longest] = (place[longest] + 1) % shape[longest]
    return drawn.at[tuple(place)].set(top_value)


def level_of(rng, shape, pieces, smallest, largest):
    level, own = 1.0, jax.random.fold_in(rng, 6)
    for axis_at, shards_of in pieces:
        draws = jnp.exp(jax.random.uniform(jax.random.fold_in(own, axis_at), (shards_of,), jnp.float32, smallest / len(pieces), largest / len(pieces)))
        level = level * jnp.repeat(draws, shape[axis_at] // shards_of).reshape([-1 if axis == axis_at else 1 for axis in range(len(shape))])
    return level


def centred(key, extent, deviation, most, pieces=(), kind=jnp.bfloat16):
    drawn = jax.random.normal(key, extent, jnp.float32) * deviation
    if len(pieces) > 0:
        drawn = level_of(key, extent, pieces, -0.22, 0.18) * drawn
    return jnp.clip(drawn, min=-most, max=most).astype(kind)


def setup_inputs(seed: int = 0) -> dict:
    arg_keys = jax.random.split(jax.random.key(seed), 9)
    x_blocks = centred(arg_keys[0], (NI, BLK, PIECES * W * BLK), 1.0, 6.0, ((0, 8), (2, 32)))
    x_cols = draw_x_cols(jax.random.fold_in(arg_keys[8], 71), 0)
    x_scales = touch_ends(jax.random.randint(arg_keys[2], (NI, PIECES * W), 0, NSCALE), jax.random.fold_in(arg_keys[2], 1), 0, NSCALE - 1).astype(jnp.int32)
    x_counts = draw_x_counts(jax.random.fold_in(arg_keys[8], 71), 0)
    scale_table = jnp.clip(jnp.exp(jax.random.uniform(arg_keys[4], (NSCALE,), jnp.float32, math.log(0.25), math.log(4.0))), 0.25, 4.0)
    s_panel = centred(arg_keys[5], (N_COL, N_LAYER, W * BLK, NJ * BLK), (W * BLK * N_COL * N_LAYER) ** -0.5, 0.09375, ((0, 8), (1, 2), (3, 16)))
    s_rows = draw_s_rows(jax.random.fold_in(arg_keys[8], 71), 0)
    s_counts = draw_s_counts(jax.random.fold_in(arg_keys[8], 71), 0)
    return dict(x_blocks=x_blocks, x_cols=x_cols, x_scales=x_scales, x_counts=x_counts, scale_table=scale_table, s_panel=s_panel, s_rows=s_rows, s_counts=s_counts)


def expand_piece(blocks, columns, scales, counts, scale_table):
    row_blocks = blocks.shape[0]
    slot_count = columns.shape[1]
    levels = scale_table.shape[0]
    matches = scales[:, :, None] == jnp.arange(levels, dtype=jnp.int32)[None, None, :]
    factors = jnp.sum(jnp.where(matches, scale_table[None, None, :], jnp.float32(0.0)), axis=2)
    is_live = jnp.arange(slot_count, dtype=jnp.int32)[None, :] < counts[:, None]
    factors = jnp.where(is_live, factors, jnp.float32(0.0))
    spread = jnp.repeat(factors, BLK, axis=1)
    scaled = (blocks.astype(jnp.float32) * spread[:, None, :]).astype(jnp.bfloat16)
    offsets = jnp.tile(jnp.arange(BLK, dtype=jnp.int32), slot_count)
    positions = jnp.repeat(columns, BLK, axis=1) * BLK + offsets[None, :]
    expansion = positions[:, :, None] == jnp.arange(KPB * BLK, dtype=jnp.int32)[None, None, :]
    dense_tiles = jnp.einsum("raj,rjk->rak", scaled.astype(jnp.float32), expansion.astype(jnp.float32))
    return dense_tiles.astype(jnp.bfloat16).reshape(row_blocks * BLK, KPB * BLK)


def densify_right(blocks, rows, counts):
    slot_count = rows.shape[0]
    col_blocks = rows.shape[1]
    is_live = jnp.arange(slot_count, dtype=jnp.int32)[:, None] < counts[None, :]
    shaped = blocks.astype(jnp.float32).reshape(slot_count, BLK, col_blocks, BLK)
    masked = jnp.where(is_live[:, None, :, None], shaped, jnp.float32(0.0))
    positions = rows[:, None, :] * BLK + jnp.arange(BLK, dtype=jnp.int32)[None, :, None]
    expansion = (positions[:, :, :, None] == jnp.arange(KPB * BLK, dtype=jnp.int32)[None, None, None, :]).astype(jnp.float32)
    dense = jnp.einsum("wajk,wajb->kjb", expansion, masked)
    return dense.reshape(KPB * BLK, col_blocks * BLK).astype(jnp.bfloat16)


def reference(x_blocks, x_cols, x_scales, x_counts, scale_table, s_panel, s_rows, s_counts):
    piece_total = N_COL * N_LAYER
    slab = W * BLK
    s_all = s_panel.reshape(piece_total, W * BLK, NJ * BLK)
    rows_all = s_rows.reshape(piece_total, W, NJ)
    counts_all = s_counts.reshape(piece_total, NJ)

    def accumulate(running, piece_index):
        blocks = lax.dynamic_slice_in_dim(x_blocks, piece_index * slab, slab, 2)
        columns = lax.dynamic_slice_in_dim(x_cols, piece_index * W, W, 1)
        scales = lax.dynamic_slice_in_dim(x_scales, piece_index * W, W, 1)
        counts = lax.dynamic_slice_in_dim(x_counts, piece_index, 1, 1)[:, 0]
        dense_piece = expand_piece(blocks, columns, scales, counts, scale_table)
        right_rows = densify_right(lax.dynamic_index_in_dim(s_all, piece_index, 0, keepdims=False), lax.dynamic_index_in_dim(rows_all, piece_index, 0, keepdims=False), lax.dynamic_index_in_dim(counts_all, piece_index, 0, keepdims=False))
        return running + jnp.dot(dense_piece, right_rows, preferred_element_type=jnp.float32), None

    initial = jnp.zeros((NI * BLK, NJ * BLK), jnp.float32)
    running, _ = lax.scan(accumulate, initial, jnp.arange(piece_total, dtype=jnp.int32))
    return running.astype(jnp.bfloat16)
```

```python
import jax
import jax.numpy as jnp
from jax import lax
from jax.experimental import pallas as pl
from jax.experimental.pallas import tpu as pltpu
from jax.sharding import PartitionSpec as P

BLK = 64
KPB = 4
LEVELS = 16
ROWS = 1024
CUT = 512
XMSG = ROWS + 16
SROWS = 256
SMSG = SROWS + 16
COLS = 256
TILE = 512
N_SEND = 96
MESH = pl.DeviceIdType.MESH


def gray(i):
    return i + i // 2 - 2 * (i // 3)


def kernel(
    x_ref, xc_ref, xs_ref, xn_ref, tab_ref, s_ref, sr_ref, sn_ref, out_ref,
    xg, xo, sg, sdu, acc, xd, fac, col, codes, send_sem, xsem, ssem,
):
    z = lax.axis_index("row")
    c = lax.axis_index("col")
    l = lax.axis_index("layer")
    k = c % 2
    x = (c // 2) % 4
    y = (c // 8) * 2 + l
    xr, xl, xx = (x + 1) % 4, (x + 3) % 4, (x + 2) % 4
    yr, yl, yy = (y + 1) % 4, (y + 3) % 4, (y + 2) % 4
    yp = (y // 2) * 2 + (1 - l)
    ks = 1 - k

    def dev(x_, y_, z_, k_):
        return (z_, (y_ // 2) * 8 + x_ * 2 + k_, y_ % 2)

    def unit(x_, y_):
        return ((y_ // 2) * 4 + x_) * 2 + y_ % 2

    def slot(x_, y_):
        return unit(x_, y_) * 2 + k

    def zat(step):
        return (z + step + 8) % 8

    right, left, sib = dev(xr, y, z, k), dev(xl, y, z, k), dev(x, y, z, ks)
    up, down = dev(x, y, zat(1), k), dev(x, y, zat(-1), k)
    ynext, yprev, yfar = dev(x, yr, z, k), dev(x, yl, z, k), dev(x, yy, z, k)
    ypair = dev(x, yp, z, k)

    barrier = pltpu.get_barrier_semaphore()
    partners = (right, left, sib, up, down, ynext, yprev, yfar)
    for other in partners:
        pl.semaphore_signal(barrier, inc=1, device_id=other, device_id_type=MESH)

    pending = []

    def send(src, dst, recv, target):
        copy = pltpu.make_async_remote_copy(
            src_ref=src, dst_ref=dst, send_sem=send_sem.at[len(pending)], recv_sem=recv,
            device_id=target, device_id_type=MESH,
        )
        copy.start()
        pending.append(copy)

    def half(ref, h):
        return ref.at[pl.ds(0, CUT)] if h == 0 else ref.at[pl.ds(CUT, XMSG - CUT)]

    def xview(s, h):
        return half(xg.at[s], h)

    def xsend(s, h, target):
        send(xview(s, h), xview(s, h), xsem.at[s * 2 + h], target)

    def xrecv(s, h):
        pltpu.make_async_remote_copy(
            src_ref=xview(s, h), dst_ref=xview(s, h), send_sem=send_sem.at[0],
            recv_sem=xsem.at[s * 2 + h], device_id=sib, device_id_type=MESH,
        ).wait_recv()

    def ssend(u, target):
        send(sg.at[u], sg.at[u], ssem.at[u], target)

    def srecv(u):
        pltpu.make_async_remote_copy(
            src_ref=sg.at[u], dst_ref=sg.at[u], send_sem=send_sem.at[0],
            recv_sem=ssem.at[u], device_id=sib, device_id_type=MESH,
        ).wait_recv()

    own_s = z * 2 + l
    lane_block = lax.broadcasted_iota(jnp.int32, (16, COLS), 1) // BLK
    list_row = lax.broadcasted_iota(jnp.int32, (16, COLS), 0)
    rows = jnp.zeros((16, COLS), jnp.int32)
    live = jnp.zeros((16, COLS), jnp.int32)
    for j in range(2):
        for b in range(COLS // BLK):
            here = lane_block == b
            live = jnp.where(here & (list_row // 2 == j), sn_ref[j, 0, b], live)
            for w in range(2):
                rows = jnp.where(here & (list_row == 2 * j + w), sr_ref[j, 0, w, b], rows)
    rows = jnp.where(list_row % 2 < live, rows, KPB)
    sg[own_s, pl.ds(0, 128), :] = s_ref[0, 0]
    sg[own_s, pl.ds(128, 128), :] = s_ref[1, 0]
    sg[own_s, pl.ds(SROWS, 16), :] = rows.astype(jnp.float32).astype(jnp.bfloat16)

    slot_of_lane = lax.broadcasted_iota(jnp.int32, (32, 128), 1) // BLK
    first = slot_of_lane == 0
    entry = jnp.where(first, xs_ref[:, 0:1], xs_ref[:, 1:2])
    factor = jnp.zeros((32, 128), jnp.float32)
    for t in range(LEVELS):
        factor = jnp.where(entry == t, tab_ref[t], factor)
    fac[...] = jnp.where(slot_of_lane < xn_ref[:, 0:1], factor, 0.0)
    col[...] = jnp.where(first, xc_ref[:, 0:1], xc_ref[:, 1:2]).astype(jnp.float32)

    def fill(dst, which):
        def row(i, carry):
            at = which * 16 + i
            scaled = x_ref[at].astype(jnp.float32) * fac[pl.ds(at, 1), :]
            dst[pl.ds(pl.multiple_of(i * BLK, BLK), BLK), :] = scaled.astype(jnp.bfloat16)
            return carry

        lax.fori_loop(0, 16, row, 0)
        dst[pl.ds(ROWS, 16), :] = col[pl.ds(pl.multiple_of(which * 16, 16), 16), :].astype(jnp.bfloat16)

    own = slot(x, y)
    fill(xg.at[own], l)
    pl.semaphore_wait(barrier, len(partners))

    ssend(own_s, ypair)
    for h in range(2):
        xsend(own, h, right)
        xsend(own, 1 - h, left)
    ssend(own_s, up)
    ssend(own_s, down)
    fill(xo, 1 - l)
    for h in range(2):
        send(half(xo, h), xview(own, h), xsem.at[own * 2 + h], ynext)
        send(half(xo, h), xview(own, h), xsem.at[own * 2 + h], yprev)
    for h in range(2):
        xsend(own, h, sib)

    def s_at(step, layer):
        return zat(step) * 2 + layer

    def s_ring(distance, layer):
        below, above = s_at(-distance, layer), s_at(distance, layer)
        srecv(below)
        ssend(below, up)
        srecv(above)
        ssend(above, down)

    def x_first(y_):
        a, b = slot(xl, y_), slot(xr, y_)
        xrecv(a, 0)
        xsend(a, 0, right)
        xrecv(b, 1)
        xsend(b, 1, left)
        xsend(a, 0, sib)
        xsend(b, 1, sib)

    def x_second(y_):
        a, b = slot(xl, y_), slot(xr, y_)
        xrecv(a, 1)
        xsend(a, 1, sib)
        xrecv(b, 0)
        xsend(b, 0, sib)

    def x_column(y_):
        s = slot(x, y_)
        xrecv(s, 0)
        xsend(s, 0, right)
        xrecv(s, 1)
        xsend(s, 1, left)
        xsend(s, 1, right)
        xsend(s, 0, left)
        for h in range(2):
            xsend(s, h, sib)

    other_s = z * 2 + (1 - l)
    srecv(other_s)
    ssend(other_s, up)
    ssend(other_s, down)
    s_ring(1, l)
    x_first(y)
    x_column(yr)
    x_column(yl)
    for h in range(2):
        xsend(own, h, yfar)
    s_ring(1, 1 - l)
    x_second(y)
    s_ring(2, l)
    x_first(yr)
    s_ring(2, 1 - l)
    x_first(yl)
    x_column(yy)
    srecv(s_at(-3, 0))
    ssend(s_at(-3, 0), up)
    srecv(s_at(3, 1))
    ssend(s_at(3, 1), down)
    srecv(s_at(-3, 1))
    srecv(s_at(3, 0))
    x_second(yr)
    x_second(yl)
    srecv(s_at(4, 0))
    srecv(s_at(4, 1))
    x_first(yy)
    x_second(yy)

    acc[...] = jnp.zeros_like(acc)
    lane_half = lax.broadcasted_iota(jnp.int32, (1, 128), 1) // BLK

    def process(u):
        for j in range(2):
            r0 = sg[u, pl.ds(SROWS, 16), :].astype(jnp.float32)
            for kb in range(KPB):
                m0 = jnp.where(r0[2 * j : 2 * j + 1] == kb, 1.0, 0.0).astype(jnp.bfloat16)
                m1 = jnp.where(r0[2 * j + 1 : 2 * j + 2] == kb, 1.0, 0.0).astype(jnp.bfloat16)
                sdu[pl.ds(j * 256 + kb * BLK, BLK), :] = (
                    sg[u, pl.ds(j * 128, BLK), :] * m0 + sg[u, pl.ds(j * 128 + BLK, BLK), :] * m1
                )
            codes[j] = xg[u * 2 + j, pl.ds(ROWS, 16), :].astype(jnp.float32)

        def tile(t, carry):
            for j in range(2):
                for i in range(TILE // BLK):
                    at = pl.multiple_of(t * TILE + i * BLK, BLK)
                    block = xg[u * 2 + j, pl.ds(at, BLK), :]
                    code = codes[j, pl.ds(t * (TILE // BLK) + i, 1), :]
                    turned = pltpu.roll(block, BLK, 1)
                    turned_code = pltpu.roll(code, BLK, 1)
                    for q in range(2):
                        want = (lane_half + 2 * q).astype(jnp.float32)
                        m0 = jnp.where(code == want, 1.0, 0.0).astype(jnp.bfloat16)
                        m1 = jnp.where(turned_code == want, 1.0, 0.0).astype(jnp.bfloat16)
                        xd[pl.ds(i * BLK, BLK), pl.ds(j * 256 + q * 128, 128)] = block * m0 + turned * m1
            out = pl.ds(pl.multiple_of(t * TILE, TILE), TILE)
            acc[out, :] += jnp.dot(xd[...], sdu[...], preferred_element_type=jnp.float32)
            return carry

        lax.fori_loop(0, ROWS // TILE, tile, 0)

    base = len(pending)

    def far_send(i, h):
        s = slot(xx, (y + gray(i)) % 4)
        return pltpu.make_async_remote_copy(
            src_ref=xview(s, h), dst_ref=xview(s, h), send_sem=send_sem.at[base + i * 2 + h],
            recv_sem=xsem.at[s * 2 + h], device_id=sib, device_id_type=MESH,
        )

    def step(j, carry):
        @pl.when((j >= 11) & (j < 15))
        def _():
            s = slot(xx, (y + gray(j - 11)) % 4)
            for h in range(2):
                xrecv(s, h)
                far_send(j - 11, h).start()

        u = unit((x + gray(j // 4)) % 4, (y + gray(j % 4)) % 4)
        for h in range(2):
            xrecv(u * 2 + ks, h)
        process(u)
        return carry

    lax.fori_loop(0, 16, step, 0)
    out_ref[...] = acc[...].astype(jnp.bfloat16)
    for copy in pending:
        copy.wait_send()
    for i in range(4):
        for h in range(2):
            far_send(i, h).wait_send()


def on_device(x_blocks, x_cols, x_scales, x_counts, scale_table, s_panel, s_rows, s_counts):
    vmem = pl.BlockSpec(memory_space=pltpu.VMEM)
    smem = pl.BlockSpec(memory_space=pltpu.SMEM)
    return pl.pallas_call(
        kernel,
        out_shape=jax.ShapeDtypeStruct((ROWS, COLS), jnp.bfloat16),
        in_specs=[vmem, vmem, vmem, vmem, smem, vmem, smem, smem],
        out_specs=vmem,
        scratch_shapes=[
            pltpu.VMEM((32, XMSG, 128), jnp.bfloat16),
            pltpu.VMEM((XMSG, 128), jnp.bfloat16),
            pltpu.VMEM((16, SMSG, COLS), jnp.bfloat16),
            pltpu.VMEM((512, COLS), jnp.bfloat16),
            pltpu.VMEM((ROWS, COLS), jnp.float32),
            pltpu.VMEM((TILE, 512), jnp.bfloat16),
            pltpu.VMEM((32, 128), jnp.float32),
            pltpu.VMEM((32, 128), jnp.float32),
            pltpu.VMEM((2, 16, 128), jnp.float32),
            pltpu.SemaphoreType.DMA((N_SEND,)),
            pltpu.SemaphoreType.DMA((64,)),
            pltpu.SemaphoreType.DMA((16,)),
        ],
        compiler_params=pltpu.CompilerParams(
            collective_id=0, has_side_effects=True, vmem_limit_bytes=40 * 1024 * 1024
        ),
        cost_estimate=pl.CostEstimate(flops=2 * 2048 * 256 * 4096, bytes_accessed=2 << 20, transcendentals=0),
    )(x_blocks, x_cols, x_scales, x_counts, scale_table, s_panel, s_rows, s_counts)


def solution(mesh):
    in_specs = (
        P("row", None, ("col", "layer")),
        P("row", ("col", "layer")),
        P("row", ("col", "layer")),
        P("row", ("col", "layer")),
        P(),
        P("row", "layer", None, "col"),
        P("row", "layer", None, "col"),
        P("row", "layer", "col"),
    )
    out_specs = P(("row", "layer"), "col")
    return jax.shard_map(
        on_device, mesh=mesh, in_specs=in_specs, out_specs=out_specs, check_vma=False
    )
```

```python
import jax
import jax.numpy as jnp
from jax import lax
from jax.experimental import pallas as pl
from jax.experimental.pallas import tpu as pltpu
from jax.sharding import PartitionSpec as P

BLK = 64
KPB = 4
LEVELS = 16
ROWS = 1024
CUT = 512
XMSG = ROWS + 16
SROWS = 256
SMSG = SROWS + 16
COLS = 256
TILE = 512
N_SEND = 96
MESH = pl.DeviceIdType.MESH


def kernel(
    x_in, xc_in, xs_in, xn_in, tab_in, s_in, sr_in, sn_in, out_ref,
    xg, xo, sg, sdu, acc, xd, codes, x_ref, s_ref, xc_ref, xs_ref, xn_ref, tab_ref, sr_ref, sn_ref,
    send_sem, xsem, ssem, in_sem,
):
    z = lax.axis_index("row")
    c = lax.axis_index("col")
    l = lax.axis_index("layer")
    k = c % 2
    x = (c // 2) % 4
    y = (c // 8) * 2 + l
    xr, xl, xx = (x + 1) % 4, (x + 3) % 4, (x + 2) % 4
    yr, yl, yy = (y + 1) % 4, (y + 3) % 4, (y + 2) % 4
    yp = (y // 2) * 2 + (1 - l)
    ks = 1 - k

    def dev(x_, y_, z_, k_):
        return (z_, (y_ // 2) * 8 + x_ * 2 + k_, y_ % 2)

    def unit(x_, y_):
        return ((y_ // 2) * 4 + x_) * 2 + y_ % 2

    def slot(x_, y_):
        return unit(x_, y_) * 2 + k

    def zat(step):
        return (z + step + 8) % 8

    right, left, sib = dev(xr, y, z, k), dev(xl, y, z, k), dev(x, y, z, ks)
    up, down = dev(x, y, zat(1), k), dev(x, y, zat(-1), k)
    ynext, yprev, yfar = dev(x, yr, z, k), dev(x, yl, z, k), dev(x, yy, z, k)
    ypair = dev(x, yp, z, k)

    barrier = pltpu.get_barrier_semaphore()
    partners = (right, left, sib, up, down, ynext, yprev, yfar)
    for other in partners:
        pl.semaphore_signal(barrier, inc=1, device_id=other, device_id_type=MESH)

    pending = []

    def send(src, dst, recv, target):
        copy = pltpu.make_async_remote_copy(
            src_ref=src, dst_ref=dst, send_sem=send_sem.at[len(pending)], recv_sem=recv,
            device_id=target, device_id_type=MESH,
        )
        copy.start()
        pending.append(copy)

    def half(ref, h):
        return ref.at[pl.ds(0, CUT)] if h == 0 else ref.at[pl.ds(CUT, XMSG - CUT)]

    def xview(s, h):
        return half(xg.at[s], h)

    def xsend(s, h, target):
        send(xview(s, h), xview(s, h), xsem.at[s * 2 + h], target)

    def xrecv(s, h):
        pltpu.make_async_remote_copy(
            src_ref=xview(s, h), dst_ref=xview(s, h), send_sem=send_sem.at[0],
            recv_sem=xsem.at[s * 2 + h], device_id=sib, device_id_type=MESH,
        ).wait_recv()

    def ssend(u, target):
        send(sg.at[u], sg.at[u], ssem.at[u], target)

    def srecv(u):
        pltpu.make_async_remote_copy(
            src_ref=sg.at[u], dst_ref=sg.at[u], send_sem=send_sem.at[0],
            recv_sem=ssem.at[u], device_id=sib, device_id_type=MESH,
        ).wait_recv()

    copies = [
        pltpu.make_async_copy(src, dst, in_sem.at[i])
        for i, (src, dst) in enumerate((
            (xc_in, xc_ref), (xs_in, xs_ref), (xn_in, xn_ref), (tab_in, tab_ref),
            (sr_in, sr_ref), (sn_in, sn_ref), (x_in, x_ref), (s_in, s_ref),
        ))
    ]
    for copy in copies:
        copy.start()
    for copy in copies:
        copy.wait()

    lane = lax.broadcasted_iota(jnp.int32, (1, 128), 1)
    list_row = lax.broadcasted_iota(jnp.int32, (16, 128), 0)
    list_first = lax.broadcasted_iota(jnp.int32, (16, 128), 1) < BLK

    def fill(dst, which):
        def row(i, cols):
            for i4 in range(4):
                r = i * 4 + i4
                at = which * 16 + r
                count = xn_ref[0, at]
                f0 = jnp.where(count > 0, tab_ref[xs_ref[0, at]], 0.0)
                f1 = jnp.where(count > 1, tab_ref[xs_ref[1, at]], 0.0)
                scaled = x_ref[at].astype(jnp.float32) * jnp.where(lane < BLK, f0, f1)
                dst[pl.ds(pl.multiple_of(r * BLK, BLK), BLK), :] = scaled.astype(jnp.bfloat16)
                cols = jnp.where(list_row == r, jnp.where(list_first, xc_ref[0, at], xc_ref[1, at]), cols)
            return cols

        cols = lax.fori_loop(0, 4, row, jnp.zeros((16, 128), jnp.int32))
        dst[pl.ds(ROWS, 16), :] = cols.astype(jnp.float32).astype(jnp.bfloat16)

    own = slot(x, y)
    fill(xg.at[own], l)

    own_s = z * 2 + l
    other_s = z * 2 + (1 - l)
    s_block = lax.broadcasted_iota(jnp.int32, (16, COLS), 1) // BLK
    s_row = lax.broadcasted_iota(jnp.int32, (16, COLS), 0)
    rows = jnp.full((16, COLS), KPB, jnp.int32)
    for j in range(2):
        for b in range(COLS // BLK):
            for w in range(2):
                live_row = jnp.where(w < sn_ref[j, 0, b], sr_ref[j, 0, w, b], KPB)
                rows = jnp.where((s_block == b) & (s_row == 2 * j + w), live_row, rows)
    sg[own_s, pl.ds(0, 128), :] = s_ref[0, 0]
    sg[own_s, pl.ds(128, 128), :] = s_ref[1, 0]
    sg[own_s, pl.ds(SROWS, 16), :] = rows.astype(jnp.float32).astype(jnp.bfloat16)

    def s_at(step, layer):
        return zat(step) * 2 + layer

    def s_ring(distance, layer):
        below, above = s_at(-distance, layer), s_at(distance, layer)
        srecv(below)
        if distance < 3 or layer is l:
            ssend(below, up)
        srecv(above)
        if distance < 3 or layer is not l:
            ssend(above, down)

    def at(e, d):
        return slot((x + e) % 4, (y + d) % 4)

    def x_first(d):
        a, b = at(3, d), at(1, d)
        xrecv(a, 0)
        xsend(a, 0, right)
        xrecv(b, 1)
        xsend(b, 1, left)
        xsend(a, 0, sib)
        xsend(b, 1, sib)

    def x_second(d):
        a, b = at(3, d), at(1, d)
        xrecv(a, 1)
        xsend(a, 1, sib)
        xrecv(b, 0)
        xsend(b, 0, sib)

    def x_column(d):
        s = at(0, d)
        xrecv(s, 0)
        xsend(s, 0, right)
        xrecv(s, 1)
        xsend(s, 1, left)
        xsend(s, 1, right)
        xsend(s, 0, left)
        for h in range(2):
            xsend(s, h, sib)

    def far_onward(d):
        s = at(2, d)
        for h in range(2):
            xrecv(s, h)
            xsend(s, h, yfar)
        for h in range(2):
            xsend(s, h, sib)

    def far_last(d):
        s = at(2, d)
        for h in range(2):
            xrecv(s, h)
            xsend(s, h, sib)

    lane_half = lax.broadcasted_iota(jnp.int32, (1, 128), 1) // BLK

    def expand(e, d):
        u = unit((x + e) % 4, (y + d) % 4)
        p = e * 4 + d
        for h in range(2):
            xrecv(u * 2 + ks, h)
        for j in range(2):
            codes[j] = xg[u * 2 + j, pl.ds(ROWS, 16), :].astype(jnp.float32)

        def rows_of(i, carry):
            for j in range(2):
                for i2 in range(2):
                    r = i * 2 + i2
                    here = pl.ds(pl.multiple_of(r * BLK, BLK), BLK)
                    block = xg[u * 2 + j, here, :]
                    code = codes[j, pl.ds(r, 1), :]
                    turned = pltpu.roll(block, BLK, 1)
                    turned_code = pltpu.roll(code, BLK, 1)
                    for q in range(2):
                        want = (lane_half + 2 * q).astype(jnp.float32)
                        m0 = jnp.where(code == want, 1.0, 0.0).astype(jnp.bfloat16)
                        m1 = jnp.where(turned_code == want, 1.0, 0.0).astype(jnp.bfloat16)
                        xd[p, here, pl.ds(j * 256 + q * 128, 128)] = block * m0 + turned * m1
            return carry

        lax.fori_loop(0, ROWS // BLK // 2, rows_of, 0)

    def multiply(e, d):
        u = unit((x + e) % 4, (y + d) % 4)
        p = e * 4 + d
        for j in range(2):
            r0 = sg[u, pl.ds(SROWS, 16), :].astype(jnp.float32)
            for kb in range(KPB):
                m0 = jnp.where(r0[2 * j : 2 * j + 1] == kb, 1.0, 0.0).astype(jnp.bfloat16)
                m1 = jnp.where(r0[2 * j + 1 : 2 * j + 2] == kb, 1.0, 0.0).astype(jnp.bfloat16)
                sdu[pl.ds(j * 256 + kb * BLK, BLK), :] = (
                    sg[u, pl.ds(j * 128, BLK), :] * m0 + sg[u, pl.ds(j * 128 + BLK, BLK), :] * m1
                )

        def tile(t, carry):
            here = pl.ds(pl.multiple_of(t * TILE, TILE), TILE)
            acc[here, :] += jnp.dot(xd[p, here, :], sdu[...], preferred_element_type=jnp.float32)
            return carry

        lax.fori_loop(0, ROWS // TILE, tile, 0)

    pl.semaphore_wait(barrier, len(partners))

    for h in range(2):
        xsend(own, h, right)
        xsend(own, 1 - h, left)
    ssend(own_s, up)
    ssend(own_s, down)
    fill(xo, 1 - l)
    for h in range(2):
        send(half(xo, h), xview(own, h), xsem.at[own * 2 + h], ynext)
        send(half(xo, h), xview(own, h), xsem.at[own * 2 + h], yprev)
    ssend(own_s, ypair)
    for h in range(2):
        xsend(own, h, sib)
    acc[...] = jnp.zeros_like(acc)

    x_first(0)
    s_ring(1, l)
    x_column(1)
    x_second(0)
    for h in range(2):
        xsend(own, h, yfar)
    s_ring(2, l)
    far_onward(0)
    srecv(other_s)
    ssend(other_s, up)
    ssend(other_s, down)
    expand(0, 0)
    expand(1, 0)
    expand(3, 0)
    x_first(1)
    x_column(3)
    s_ring(3, l)
    other = 1 - l
    s_ring(1, other)
    expand(0, 1)
    expand(0, 3)
    expand(2, 0)
    x_column(2)
    s_ring(2, other)
    x_second(1)
    far_last(2)
    far_onward(1)
    srecv(s_at(4, l))
    s_ring(3, other)
    expand(0, 2)
    expand(1, 1)
    expand(3, 1)
    expand(2, 2)
    expand(2, 1)
    srecv(s_at(4, other))

    def own_column(i, carry):
        multiply(0, i)
        return carry

    def beside(i, carry):
        multiply(1 + 2 * (i % 2), i // 2)
        return carry

    def far_column(i, carry):
        multiply(2, i)
        return carry

    base = len(pending)
    N_LATE = 5

    def late_at(i):
        m = i % 3
        return 1 + 2 * m - 3 * (m // 2), 3 - i // 3

    def late_send(i, h):
        s = at(*late_at(i))
        return pltpu.make_async_remote_copy(
            src_ref=xview(s, h), dst_ref=xview(s, h), send_sem=send_sem.at[base + i * 2 + h],
            recv_sem=xsem.at[s * 2 + h], device_id=sib, device_id_type=MESH,
        )

    def late_take(i):
        for h in range(2):
            xrecv(at(*late_at(i)), h)
            late_send(i, h).start()

    lax.fori_loop(0, 4, own_column, 0)
    late_take(0)
    late_take(1)
    lax.fori_loop(0, 4, beside, 0)
    lax.fori_loop(0, 3, far_column, 0)

    def late(i, carry):
        expand(*late_at(i))
        multiply(*late_at(i))

        @pl.when(i + 2 < N_LATE)
        def _():
            late_take(i + 2)

        return carry

    lax.fori_loop(0, N_LATE, late, 0)
    out_ref[...] = acc[...].astype(jnp.bfloat16)
    for copy in pending:
        copy.wait_send()
    for i in range(N_LATE):
        for h in range(2):
            late_send(i, h).wait_send()


def on_device(x_blocks, x_cols, x_scales, x_counts, scale_table, s_panel, s_rows, s_counts):
    hbm = pl.BlockSpec(memory_space=pltpu.HBM)
    return pl.pallas_call(
        kernel,
        out_shape=jax.ShapeDtypeStruct((ROWS, COLS), jnp.bfloat16),
        in_specs=[hbm] * 8,
        out_specs=pl.BlockSpec(memory_space=pltpu.VMEM),
        scratch_shapes=[
            pltpu.VMEM((32, XMSG, 128), jnp.bfloat16),
            pltpu.VMEM((XMSG, 128), jnp.bfloat16),
            pltpu.VMEM((16, SMSG, COLS), jnp.bfloat16),
            pltpu.VMEM((512, COLS), jnp.bfloat16),
            pltpu.VMEM((ROWS, COLS), jnp.float32),
            pltpu.VMEM((16, ROWS, 512), jnp.bfloat16),
            pltpu.VMEM((2, 16, 128), jnp.float32),
            pltpu.VMEM((32, BLK, 128), jnp.bfloat16),
            pltpu.VMEM((2, 1, 128, COLS), jnp.bfloat16),
            pltpu.SMEM((2, 32), jnp.int32),
            pltpu.SMEM((2, 32), jnp.int32),
            pltpu.SMEM((1, 32), jnp.int32),
            pltpu.SMEM((LEVELS,), jnp.float32),
            pltpu.SMEM((2, 1, 2, 4), jnp.int32),
            pltpu.SMEM((2, 1, 4), jnp.int32),
            pltpu.SemaphoreType.DMA((N_SEND,)),
            pltpu.SemaphoreType.DMA((64,)),
            pltpu.SemaphoreType.DMA((16,)),
            pltpu.SemaphoreType.DMA((8,)),
        ],
        compiler_params=pltpu.CompilerParams(
            collective_id=0, has_side_effects=True, vmem_limit_bytes=48 * 1024 * 1024
        ),
        cost_estimate=pl.CostEstimate(flops=2 * 2048 * 256 * 4096, bytes_accessed=2 << 20, transcendentals=0),
    )(x_blocks, x_cols.T, x_scales.T, x_counts.T, scale_table, s_panel, s_rows, s_counts)


def solution(mesh):
    in_specs = (
        P("row", None, ("col", "layer")),
        P("row", ("col", "layer")),
        P("row", ("col", "layer")),
        P("row", ("col", "layer")),
        P(),
        P("row", "layer", None, "col"),
        P("row", "layer", None, "col"),
        P("row", "layer", "col"),
    )
    out_specs = P(("row", "layer"), "col")
    return jax.shard_map(
        on_device, mesh=mesh, in_specs=in_specs, out_specs=out_specs, check_vma=False
    )
```

```python
import jax
import jax.numpy as jnp
from jax import lax
from jax.experimental import pallas as pl
from jax.experimental.pallas import tpu as pltpu
from jax.sharding import PartitionSpec as P

BLK = 64
KPB = 4
LEVELS = 16
ROWS = 1024
CUT = 512
XMSG = ROWS + 16
SROWS = 256
SMSG = SROWS + 16
COLS = 256
TILE = 256
LATE_TILE = 512
N_SEND = 96
MESH = pl.DeviceIdType.MESH


def kernel(
    x_in, xc_in, xs_in, xn_in, tab_in, s_in, sr_in, sn_in, out_ref,
    xg, xo, sg, sd, acc, xd, codes, x_ref, s_ref, xc_ref, xs_ref, xn_ref, tab_ref, sr_ref, sn_ref,
    send_sem, xsem, ssem, in_sem,
):
    z = lax.axis_index("row")
    c = lax.axis_index("col")
    l = lax.axis_index("layer")
    k = c % 2
    x = (c // 2) % 4
    y = (c // 8) * 2 + l
    xr, xl, xx = (x + 1) % 4, (x + 3) % 4, (x + 2) % 4
    yr, yl, yy = (y + 1) % 4, (y + 3) % 4, (y + 2) % 4
    yp = (y // 2) * 2 + (1 - l)
    ks = 1 - k

    def dev(x_, y_, z_, k_):
        return (z_, (y_ // 2) * 8 + x_ * 2 + k_, y_ % 2)

    def unit(x_, y_):
        return ((y_ // 2) * 4 + x_) * 2 + y_ % 2

    def slot(x_, y_):
        return unit(x_, y_) * 2 + k

    def zat(step):
        return (z + step + 8) % 8

    right, left, sib = dev(xr, y, z, k), dev(xl, y, z, k), dev(x, y, z, ks)
    up, down = dev(x, y, zat(1), k), dev(x, y, zat(-1), k)
    ynext, yprev, yfar = dev(x, yr, z, k), dev(x, yl, z, k), dev(x, yy, z, k)
    ypair = dev(x, yp, z, k)

    barrier = pltpu.get_barrier_semaphore()
    partners = (right, left, sib, up, down, ynext, yprev, yfar)
    for other in partners:
        pl.semaphore_signal(barrier, inc=1, device_id=other, device_id_type=MESH)

    pending = []

    def send(src, dst, recv, target):
        copy = pltpu.make_async_remote_copy(
            src_ref=src, dst_ref=dst, send_sem=send_sem.at[len(pending)], recv_sem=recv,
            device_id=target, device_id_type=MESH,
        )
        copy.start()
        pending.append(copy)

    def half(ref, h):
        return ref.at[pl.ds(0, CUT)] if h == 0 else ref.at[pl.ds(CUT, XMSG - CUT)]

    def xview(s, h):
        return half(xg.at[s], h)

    def xsend(s, h, target):
        send(xview(s, h), xview(s, h), xsem.at[s * 2 + h], target)

    def xrecv(s, h):
        pltpu.make_async_remote_copy(
            src_ref=xview(s, h), dst_ref=xview(s, h), send_sem=send_sem.at[0],
            recv_sem=xsem.at[s * 2 + h], device_id=sib, device_id_type=MESH,
        ).wait_recv()

    def ssend(u, target):
        send(sg.at[u], sg.at[u], ssem.at[u], target)

    def srecv(u):
        pltpu.make_async_remote_copy(
            src_ref=sg.at[u], dst_ref=sg.at[u], send_sem=send_sem.at[0],
            recv_sem=ssem.at[u], device_id=sib, device_id_type=MESH,
        ).wait_recv()

    copies = [
        pltpu.make_async_copy(src, dst, in_sem.at[i])
        for i, (src, dst) in enumerate((
            (xc_in, xc_ref), (xs_in, xs_ref), (xn_in, xn_ref), (tab_in, tab_ref),
            (sr_in, sr_ref), (sn_in, sn_ref), (x_in, x_ref), (s_in, s_ref),
        ))
    ]
    for copy in copies:
        copy.start()
    for copy in copies:
        copy.wait()

    lane = lax.broadcasted_iota(jnp.int32, (1, 128), 1)
    list_row = lax.broadcasted_iota(jnp.int32, (16, 128), 0)
    list_first = lax.broadcasted_iota(jnp.int32, (16, 128), 1) < BLK

    def fill(dst, which):
        def row(i, cols):
            for i4 in range(4):
                r = i * 4 + i4
                at = which * 16 + r
                count = xn_ref[0, at]
                f0 = jnp.where(count > 0, tab_ref[xs_ref[0, at]], 0.0)
                f1 = jnp.where(count > 1, tab_ref[xs_ref[1, at]], 0.0)
                scaled = x_ref[at].astype(jnp.float32) * jnp.where(lane < BLK, f0, f1)
                dst[pl.ds(pl.multiple_of(r * BLK, BLK), BLK), :] = scaled.astype(jnp.bfloat16)
                cols = jnp.where(list_row == r, jnp.where(list_first, xc_ref[0, at], xc_ref[1, at]), cols)
            return cols

        cols = lax.fori_loop(0, 4, row, jnp.zeros((16, 128), jnp.int32))
        dst[pl.ds(ROWS, 16), :] = cols.astype(jnp.float32).astype(jnp.bfloat16)

    own = slot(x, y)
    fill(xg.at[own], l)

    own_s = z * 2 + l
    other_s = z * 2 + (1 - l)
    s_block = lax.broadcasted_iota(jnp.int32, (16, COLS), 1) // BLK
    s_row = lax.broadcasted_iota(jnp.int32, (16, COLS), 0)
    rows = jnp.full((16, COLS), KPB, jnp.int32)
    for j in range(2):
        for b in range(COLS // BLK):
            for w in range(2):
                live_row = jnp.where(w < sn_ref[j, 0, b], sr_ref[j, 0, w, b], KPB)
                rows = jnp.where((s_block == b) & (s_row == 2 * j + w), live_row, rows)
    sg[own_s, pl.ds(0, 128), :] = s_ref[0, 0]
    sg[own_s, pl.ds(128, 128), :] = s_ref[1, 0]
    sg[own_s, pl.ds(SROWS, 16), :] = rows.astype(jnp.float32).astype(jnp.bfloat16)

    def s_at(step, layer):
        return zat(step) * 2 + layer

    def s_ring(distance, layer):
        below, above = s_at(-distance, layer), s_at(distance, layer)
        srecv(below)
        if distance < 3 or layer is l:
            ssend(below, up)
        srecv(above)
        if distance < 3 or layer is not l:
            ssend(above, down)

    def at(e, m):
        return slot((x + e) % 4, (y + along_y(m)) % 4)

    def x_first(m):
        a, b = at(3, m), at(1, m)
        xrecv(a, 0)
        xsend(a, 0, right)
        xrecv(b, 1)
        xsend(b, 1, left)
        xsend(a, 0, sib)
        xsend(b, 1, sib)

    def x_second(m):
        a, b = at(3, m), at(1, m)
        xrecv(a, 1)
        xsend(a, 1, sib)
        xrecv(b, 0)
        xsend(b, 0, sib)

    def x_column(m):
        s = at(0, m)
        xrecv(s, 0)
        xsend(s, 0, right)
        xrecv(s, 1)
        xsend(s, 1, left)
        xsend(s, 1, right)
        xsend(s, 0, left)
        for h in range(2):
            xsend(s, h, sib)

    def far_onward(m):
        s = at(2, m)
        for h in range(2):
            xrecv(s, h)
            xsend(s, h, yfar)
        for h in range(2):
            xsend(s, h, sib)

    def late_take(e, m):
        s = at(e, m)
        for h in range(2):
            xrecv(s, h)
            xsend(s, h, sib)

    lane_half = lax.broadcasted_iota(jnp.int32, (1, 128), 1) // BLK

    near = 3 - 2 * l

    def along_y(m):
        return (m * near) % 4

    def expand(e, m):
        u = unit((x + e) % 4, (y + along_y(m)) % 4)
        first = (e * 4 + m) * 512
        for h in range(2):
            xrecv(u * 2 + ks, h)
        for j in range(2):
            codes[j] = xg[u * 2 + j, pl.ds(ROWS, 16), :].astype(jnp.float32)

        def rows_of(i, carry):
            for j in range(2):
                for i2 in range(2):
                    r = i * 2 + i2
                    here = pl.ds(pl.multiple_of(r * BLK, BLK), BLK)
                    block = xg[u * 2 + j, here, :]
                    code = codes[j, pl.ds(r, 1), :]
                    turned = pltpu.roll(block, BLK, 1)
                    turned_code = pltpu.roll(code, BLK, 1)
                    for q in range(2):
                        want = (lane_half + 2 * q).astype(jnp.float32)
                        m0 = jnp.where(code == want, 1.0, 0.0).astype(jnp.bfloat16)
                        m1 = jnp.where(turned_code == want, 1.0, 0.0).astype(jnp.bfloat16)
                        xd[here, pl.ds(first + j * 256 + q * 128, 128)] = block * m0 + turned * m1
            return carry

        lax.fori_loop(0, ROWS // BLK // 2, rows_of, 0)

    def densify(u):
        e = ((u // 2) % 4 - x + 4) % 4
        m = (((u // 8) * 2 + u % 2 - y + 4) * near) % 4
        first = (e * 4 + m) * 512
        for j in range(2):
            r0 = sg[u, pl.ds(SROWS, 16), :].astype(jnp.float32)
            for kb in range(KPB):
                m0 = jnp.where(r0[2 * j : 2 * j + 1] == kb, 1.0, 0.0).astype(jnp.bfloat16)
                m1 = jnp.where(r0[2 * j + 1 : 2 * j + 2] == kb, 1.0, 0.0).astype(jnp.bfloat16)
                sd[pl.ds(pl.multiple_of(first + j * 256 + kb * BLK, BLK), BLK), :] = (
                    sg[u, pl.ds(j * 128, BLK), :] * m0 + sg[u, pl.ds(j * 128 + BLK, BLK), :] * m1
                )

    def densify_at(distance):
        def one(i, carry):
            densify(s_at((2 * (i // 2) - 1) * distance, i % 2))
            return carry

        lax.fori_loop(0, 2 if distance in (0, 4) else 4, one, 0)

    def dot(here, ranges):
        total = None
        for first, count in ranges:
            k = pl.ds(first * 512, count * 512)
            term = jnp.dot(xd[here, k], sd[k, :], preferred_element_type=jnp.float32)
            total = term if total is None else total + term
        return total

    pl.semaphore_wait(barrier, len(partners))

    for h in range(2):
        xsend(own, h, right)
        xsend(own, 1 - h, left)
    ssend(own_s, ypair)
    ssend(own_s, up)
    ssend(own_s, down)
    fill(xo, 1 - l)
    for h in range(2):
        send(half(xo, h), xview(own, h), xsem.at[own * 2 + h], ynext)
        send(half(xo, h), xview(own, h), xsem.at[own * 2 + h], yprev)
    for h in range(2):
        xsend(own, h, sib)
    other = 1 - l
    x_first(0)
    srecv(other_s)
    ssend(other_s, up)
    ssend(other_s, down)
    s_ring(1, l)
    x_column(1)
    x_second(0)
    for h in range(2):
        xsend(own, h, yfar)
    s_ring(1, other)
    far_onward(0)
    expand(0, 0)
    expand(1, 0)
    expand(3, 0)
    x_first(1)
    x_column(3)
    s_ring(2, l)
    densify_at(0)
    densify_at(1)
    expand(0, 1)
    s_ring(2, other)
    x_second(1)
    x_column(2)
    expand(0, 3)
    expand(2, 0)
    densify_at(2)
    far_onward(1)
    s_ring(3, l)
    expand(0, 2)
    expand(1, 1)
    expand(3, 1)
    expand(2, 1)
    late_take(2, 2)
    s_ring(3, other)
    densify_at(3)
    for e in (1, 3):
        late_take(e, 3)
    expand(2, 2)
    srecv(s_at(4, l))
    srecv(s_at(4, other))
    densify_at(4)

    def early(t, carry):
        here = pl.ds(pl.multiple_of(t * TILE, TILE), TILE)
        acc[here, :] = dot(here, ((0, 4), (4, 2), (8, 3), (12, 2)))
        return carry

    lax.fori_loop(0, 2, early, 0)
    late_take(2, 3)
    lax.fori_loop(2, 4, early, 0)
    for e in (1, 3):
        late_take(e, 2)
    expand(1, 3)
    expand(3, 3)
    expand(2, 3)

    def late(t, carry):
        here = pl.ds(pl.multiple_of(t * LATE_TILE, LATE_TILE), LATE_TILE)
        acc[here, :] += dot(here, ((7, 1), (15, 1), (11, 1)))
        return carry

    lax.fori_loop(0, ROWS // LATE_TILE, late, 0)
    expand(1, 2)
    expand(3, 2)

    def last(t, carry):
        here = pl.ds(pl.multiple_of(t * LATE_TILE, LATE_TILE), LATE_TILE)
        out_ref[here, :] = (acc[here, :] + dot(here, ((6, 1), (14, 1)))).astype(jnp.bfloat16)
        return carry

    lax.fori_loop(0, ROWS // LATE_TILE, last, 0)
    for copy in pending:
        copy.wait_send()


def on_device(x_blocks, x_cols, x_scales, x_counts, scale_table, s_panel, s_rows, s_counts):
    hbm = pl.BlockSpec(memory_space=pltpu.HBM)
    return pl.pallas_call(
        kernel,
        out_shape=jax.ShapeDtypeStruct((ROWS, COLS), jnp.bfloat16),
        in_specs=[hbm] * 8,
        out_specs=pl.BlockSpec(memory_space=pltpu.VMEM),
        scratch_shapes=[
            pltpu.VMEM((32, XMSG, 128), jnp.bfloat16),
            pltpu.VMEM((XMSG, 128), jnp.bfloat16),
            pltpu.VMEM((16, SMSG, COLS), jnp.bfloat16),
            pltpu.VMEM((8192, COLS), jnp.bfloat16),
            pltpu.VMEM((ROWS, COLS), jnp.float32),
            pltpu.VMEM((ROWS, 8192), jnp.bfloat16),
            pltpu.VMEM((2, 16, 128), jnp.float32),
            pltpu.VMEM((32, BLK, 128), jnp.bfloat16),
            pltpu.VMEM((2, 1, 128, COLS), jnp.bfloat16),
            pltpu.SMEM((2, 32), jnp.int32),
            pltpu.SMEM((2, 32), jnp.int32),
            pltpu.SMEM((1, 32), jnp.int32),
            pltpu.SMEM((LEVELS,), jnp.float32),
            pltpu.SMEM((2, 1, 2, 4), jnp.int32),
            pltpu.SMEM((2, 1, 4), jnp.int32),
            pltpu.SemaphoreType.DMA((N_SEND,)),
            pltpu.SemaphoreType.DMA((64,)),
            pltpu.SemaphoreType.DMA((16,)),
            pltpu.SemaphoreType.DMA((8,)),
        ],
        compiler_params=pltpu.CompilerParams(
            collective_id=0, has_side_effects=True, vmem_limit_bytes=60 * 1024 * 1024
        ),
        cost_estimate=pl.CostEstimate(flops=2 * 2048 * 256 * 4096, bytes_accessed=2 << 20, transcendentals=0),
    )(x_blocks, x_cols.T, x_scales.T, x_counts.T, scale_table, s_panel, s_rows, s_counts)


def solution(mesh):
    in_specs = (
        P("row", None, ("col", "layer")),
        P("row", ("col", "layer")),
        P("row", ("col", "layer")),
        P("row", ("col", "layer")),
        P(),
        P("row", "layer", None, "col"),
        P("row", "layer", None, "col"),
        P("row", "layer", "col"),
    )
    out_specs = P(("row", "layer"), "col")
    return jax.shard_map(
        on_device, mesh=mesh, in_specs=in_specs, out_specs=out_specs, check_vma=False
    )
```

```python
import jax
import jax.numpy as jnp
from jax import lax
from jax.experimental import pallas as pl
from jax.experimental.pallas import tpu as pltpu
from jax.sharding import PartitionSpec as P

BLK = 64
KPB = 4
LEVELS = 16
ROWS = 1024
CUT = 512
LIST = 16
XMSG = LIST + ROWS
SROWS = 256
SMSG = SROWS + 16
COLS = 256
TILE = 256
N_SEND = 96
MESH = pl.DeviceIdType.MESH


def kernel(
    x_in, xc_in, xs_in, xn_in, tab_in, s_in, sr_in, sn_in, out_ref,
    xg, xo, sg, sd, acc, xd, outv, x_ref, s_ref, xc_ref, xs_ref, xn_ref, tab_ref, sr_ref, sn_ref,
    send_sem, xsem, ssem, in_sem,
):
    z = lax.axis_index("row")
    c = lax.axis_index("col")
    l = lax.axis_index("layer")
    k = c % 2
    x = (c // 2) % 4
    y = (c // 8) * 2 + l
    xr, xl = (x + 1) % 4, (x + 3) % 4
    near = 3 - 2 * l
    yn, yp, yy = (y + near) % 4, (y + 4 - near) % 4, (y + 2) % 4
    ks = 1 - k

    def dev(x_, y_, z_, k_):
        return (z_, (y_ // 2) * 8 + x_ * 2 + k_, y_ % 2)

    def unit(x_, y_):
        return ((y_ // 2) * 4 + x_) * 2 + y_ % 2

    def slot(x_, y_):
        return unit(x_, y_) * 2 + k

    def zat(step):
        return (z + step + 8) % 8

    right, left, sib = dev(xr, y, z, k), dev(xl, y, z, k), dev(x, y, z, ks)
    up, down = dev(x, y, zat(1), k), dev(x, y, zat(-1), k)
    ynear, ypair, yfar = dev(x, yn, z, k), dev(x, yp, z, k), dev(x, yy, z, k)

    barrier = pltpu.get_barrier_semaphore()
    partners = (right, left, sib, up, down, ynear, ypair, yfar)
    for other in partners:
        pl.semaphore_signal(barrier, inc=1, device_id=other, device_id_type=MESH)

    pending = []

    def remote(index, ends):
        src, dst, recv, target = ends()
        return pltpu.make_async_remote_copy(
            src_ref=src, dst_ref=dst, send_sem=send_sem.at[index], recv_sem=recv,
            device_id=target, device_id_type=MESH,
        )

    def send(ends):
        remote(len(pending), ends).start()
        pending.append(ends)

    def half(ref, h):
        return ref.at[pl.ds(0, LIST + CUT)] if h == 0 else ref.at[pl.ds(LIST + CUT, CUT)]

    def xview(s, h):
        return half(xg.at[s], h)

    def xrecv(s, h):
        pltpu.make_async_remote_copy(
            src_ref=xview(s, h), dst_ref=xview(s, h), send_sem=send_sem.at[0],
            recv_sem=xsem.at[s * 2 + h], device_id=sib, device_id_type=MESH,
        ).wait_recv()

    def sview(u, q):
        return sg.at[u, pl.ds(0, 128)] if q == 0 else sg.at[u, pl.ds(128, SMSG - 128)]

    def srecv(u, q):
        pltpu.make_async_remote_copy(
            src_ref=sview(u, q), dst_ref=sview(u, q), send_sem=send_sem.at[0],
            recv_sem=ssem.at[u * 2 + q], device_id=sib, device_id_type=MESH,
        ).wait_recv()

    copies = [
        pltpu.make_async_copy(src, dst, in_sem.at[i])
        for i, (src, dst) in enumerate((
            (xc_in, xc_ref), (xs_in, xs_ref), (xn_in, xn_ref), (tab_in, tab_ref),
            (sr_in, sr_ref), (sn_in, sn_ref), (x_in, x_ref), (s_in, s_ref),
        ))
    ]
    for copy in copies:
        copy.start()
    for copy in copies:
        copy.wait()

    lane = lax.broadcasted_iota(jnp.int32, (1, 128), 1)
    list_row = lax.broadcasted_iota(jnp.int32, (16, 128), 0)
    list_first = lax.broadcasted_iota(jnp.int32, (16, 128), 1) < BLK

    def fill(dst, which):
        def row(i, cols):
            for i4 in range(4):
                r = i * 4 + i4
                at = which * 16 + r
                count = xn_ref[0, at]
                f0 = jnp.where(count > 0, tab_ref[xs_ref[0, at]], 0.0)
                f1 = jnp.where(count > 1, tab_ref[xs_ref[1, at]], 0.0)
                scaled = x_ref[at].astype(jnp.float32) * jnp.where(lane < BLK, f0, f1)
                dst[pl.ds(pl.multiple_of(LIST + r * BLK, LIST), BLK), :] = scaled.astype(jnp.bfloat16)
                cols = jnp.where(list_row == r, jnp.where(list_first, xc_ref[0, at], xc_ref[1, at]), cols)
            return cols

        cols = lax.fori_loop(0, 4, row, jnp.zeros((16, 128), jnp.int32))
        dst[pl.ds(0, LIST), :] = cols.astype(jnp.float32).astype(jnp.bfloat16)

    own = slot(x, y)
    fill(xg.at[own], l)
    fill(xo, 1 - l)

    own_s = z * 2 + l
    other = 1 - l
    s_block = lax.broadcasted_iota(jnp.int32, (16, COLS), 1) // BLK
    s_row = lax.broadcasted_iota(jnp.int32, (16, COLS), 0)
    rows = jnp.full((16, COLS), KPB, jnp.int32)
    for j in range(2):
        for b in range(COLS // BLK):
            for w in range(2):
                live_row = jnp.where(w < sn_ref[j, 0, b], sr_ref[j, 0, w, b], KPB)
                rows = jnp.where((s_block == b) & (s_row == 2 * j + w), live_row, rows)
    sg[own_s, pl.ds(0, 128), :] = s_ref[0, 0]
    sg[own_s, pl.ds(128, 128), :] = s_ref[1, 0]
    sg[own_s, pl.ds(SROWS, 16), :] = rows.astype(jnp.float32).astype(jnp.bfloat16)

    def s_at(step, layer):
        return zat(step) * 2 + layer

    def at(e, m):
        return slot((x + e) % 4, (y + along_y(m)) % 4)

    def take(e, m, h):
        xrecv(at(e, m), h)

    def give(e, m, h, target):
        def ends():
            s = at(e, m)
            return xview(s, h), xview(s, h), xsem.at[s * 2 + h], target

        send(ends)

    def take_s(step, layer, q):
        srecv(s_at(step, layer), q)

    def give_s(step, layer, q, target):
        def ends():
            u = s_at(step, layer)
            return sview(u, q), sview(u, q), ssem.at[u * 2 + q], target

        send(ends)

    lane_half = lax.broadcasted_iota(jnp.int32, (LIST, 128), 1) // BLK

    def along_y(m):
        return (m * near) % 4

    def expand(e, m, start, count):
        u = unit((x + e) % 4, (y + along_y(m)) % 4)
        first = (e * 4 + m) * 512
        for h in range(start // 8, (start + count) // 8):
            xrecv(u * 2 + ks, h)
        for j in range(2):
            code = xg[u * 2 + j, pl.ds(0, LIST), :].astype(jnp.float32)
            turned_code = pltpu.roll(code, BLK, 1)
            kept, moved = [], []
            for q in range(2):
                want = (lane_half + 2 * q).astype(jnp.float32)
                kept.append(jnp.where(code == want, 1.0, 0.0).astype(jnp.bfloat16))
                moved.append(jnp.where(turned_code == want, 1.0, 0.0).astype(jnp.bfloat16))
            for r in range(start, start + count):
                block = xg[u * 2 + j, pl.ds(LIST + r * BLK, BLK), :]
                turned = pltpu.roll(block, BLK, 1)
                for q in range(2):
                    xd[pl.ds(r * BLK, BLK), pl.ds(first + j * 256 + q * 128, 128)] = (
                        block * kept[q][r : r + 1] + turned * moved[q][r : r + 1]
                    )

    def place(u):
        return ((u // 2) % 4 - x + 4) % 4, (((u // 8) * 2 + u % 2 - y + 4) * near) % 4

    def densify(u):
        e, m = place(u)
        first = (e * 4 + m) * 512
        for j in range(2):
            r0 = sg[u, pl.ds(SROWS, 16), :].astype(jnp.float32)
            for kb in range(KPB):
                m0 = jnp.where(r0[2 * j : 2 * j + 1] == kb, 1.0, 0.0).astype(jnp.bfloat16)
                m1 = jnp.where(r0[2 * j + 1 : 2 * j + 2] == kb, 1.0, 0.0).astype(jnp.bfloat16)
                sd[pl.ds(pl.multiple_of(first + j * 256 + kb * BLK, BLK), BLK), :] = (
                    sg[u, pl.ds(j * 128, BLK), :] * m0 + sg[u, pl.ds(j * 128 + BLK, BLK), :] * m1
                )

    def densify_at(distance):
        def one(i, carry):
            densify(s_at((2 * (i // 2) - 1) * distance, i % 2))
            return carry

        lax.fori_loop(0, 2 if distance in (0, 4) else 4, one, 0)

    def dot(here, ranges):
        total = None
        for first, count in ranges:
            k = pl.ds(first * 512, count * 512)
            term = jnp.dot(xd[here, k], sd[k, :], preferred_element_type=jnp.float32)
            total = term if total is None else total + term
        return total

    pl.semaphore_wait(barrier, len(partners))

    give(0, 0, 0, right)
    give(0, 0, 1, left)
    for q in range(2):
        give_s(0, l, q, ypair)
    for q in range(2):
        give_s(0, l, q, up)
        give_s(0, l, q, down)
    give(0, 0, 1, right)
    give(0, 0, 0, left)
    for h in range(2):
        for target in (ynear, ypair):
            send(lambda h=h, target=target: (half(xo, h), xview(own, h), xsem.at[own * 2 + h], target))
    for h in range(2):
        give(0, 0, h, sib)
    for h in range(2):
        give(0, 0, h, yfar)

    def clear(i, carry):
        e, m = place(s_at(4, i))
        sd[pl.ds(pl.multiple_of((e * 4 + m) * 512, 512), 512), :] = jnp.zeros((512, COLS), jnp.bfloat16)
        return carry

    lax.fori_loop(0, 2, clear, 0)

    expand(0, 0, 0, 16)
    take_s(0, other, 0)
    give_s(0, other, 0, up)
    give_s(0, other, 0, down)
    take_s(-1, l, 0)
    give_s(-1, l, 0, up)
    take_s(1, l, 0)
    give_s(1, l, 0, down)
    take(3, 0, 0)
    give(3, 0, 0, right)
    give(3, 0, 0, sib)
    take_s(0, other, 1)
    give_s(0, other, 1, up)
    give_s(0, other, 1, down)
    take_s(-1, l, 1)
    give_s(-1, l, 1, up)
    take_s(1, l, 1)
    give_s(1, l, 1, down)
    densify_at(0)
    take(0, 1, 0)
    give(0, 1, 0, right)
    give(0, 1, 0, left)
    give(0, 1, 0, sib)
    take_s(-1, other, 0)
    give_s(-1, other, 0, up)
    take_s(1, other, 0)
    give_s(1, other, 0, down)
    take(3, 0, 1)
    give(3, 0, 1, sib)
    take(1, 0, 0)
    give(1, 0, 0, sib)
    take(0, 1, 1)
    give(0, 1, 1, left)
    take(1, 0, 1)
    give(1, 0, 1, left)
    give(0, 1, 1, right)
    give(1, 0, 1, sib)
    give(0, 1, 1, sib)
    take_s(-2, l, 0)
    give_s(-2, l, 0, up)
    take_s(2, l, 0)
    give_s(2, l, 0, down)
    expand(3, 0, 0, 16)
    take_s(-1, other, 1)
    give_s(-1, other, 1, up)
    take_s(1, other, 1)
    give_s(1, other, 1, down)
    densify_at(1)
    take(2, 0, 0)
    give(2, 0, 0, yfar)
    give(2, 0, 0, sib)
    take(1, 1, 0)
    give(1, 1, 0, sib)
    expand(1, 0, 0, 16)
    expand(0, 1, 0, 16)
    take_s(-2, l, 1)
    give_s(-2, l, 1, up)
    take_s(2, l, 1)
    give_s(2, l, 1, down)
    take_s(-2, other, 0)
    give_s(-2, other, 0, up)
    take_s(2, other, 0)
    give_s(2, other, 0, down)
    take(3, 1, 0)
    give(3, 1, 0, right)
    give(3, 1, 0, sib)
    take(1, 1, 1)
    give(1, 1, 1, left)
    take(0, 3, 0)
    give(0, 3, 0, right)
    give(0, 3, 0, left)
    take(0, 3, 1)
    give(0, 3, 1, right)
    give(0, 3, 1, left)
    take(0, 2, 0)
    give(0, 2, 0, right)
    give(0, 2, 0, left)
    give(1, 1, 1, sib)
    give(0, 3, 0, sib)
    give(0, 3, 1, sib)
    give(0, 2, 0, sib)
    take_s(-3, l, 0)
    give_s(-3, l, 0, up)
    take_s(3, l, 0)
    take(0, 2, 1)
    give(0, 2, 1, right)
    give(0, 2, 1, left)
    give(0, 2, 1, sib)
    take_s(-2, other, 1)
    give_s(-2, other, 1, up)
    take_s(2, other, 1)
    give_s(2, other, 1, down)
    take(3, 1, 1)
    give(3, 1, 1, sib)
    densify_at(2)
    take(2, 0, 1)
    give(2, 0, 1, yfar)
    give(2, 0, 1, sib)
    expand(1, 1, 0, 16)
    expand(0, 3, 0, 16)
    take(2, 2, 0)
    give(2, 2, 0, sib)
    take_s(-3, l, 1)
    give_s(-3, l, 1, up)
    take_s(3, l, 1)
    expand(0, 2, 0, 16)
    expand(3, 1, 0, 16)
    expand(2, 0, 0, 16)
    take_s(-3, other, 0)
    take_s(3, other, 0)
    give_s(3, other, 0, down)
    take(2, 1, 0)
    give(2, 1, 0, yfar)
    take(2, 1, 1)
    give(2, 1, 1, yfar)
    give(2, 1, 0, sib)
    give(2, 1, 1, sib)
    take_s(-4, l, 0)
    take_s(3, other, 1)
    give_s(3, other, 1, down)
    take(3, 3, 0)
    give(3, 3, 0, sib)
    take(1, 3, 0)
    give(1, 3, 0, sib)
    take_s(-3, other, 1)
    densify_at(3)
    expand(2, 1, 0, 16)
    take(2, 2, 1)
    give(2, 2, 1, sib)

    def farthest():
        def one(i, carry):
            e, m = place(s_at(4, i))

            @pl.when((e == 0) | ((e == 2) & (m == 0)) | ((e % 2 == 1) & (m < 2)))
            def _():
                k = pl.ds(pl.multiple_of((e * 4 + m) * 512, 512), 512)
                acc[...] += jnp.dot(xd[:, k], sd[k, :], preferred_element_type=jnp.float32)

            return carry

        lax.fori_loop(0, 2, one, 0)

    def early(t, carry):
        here = pl.ds(pl.multiple_of(t * TILE, TILE), TILE)
        acc[here, :] = dot(here, ((0, 4), (4, 2), (8, 1), (12, 2)))

        @pl.when(t == 0)
        def _():
            take_s(4, other, 0)
            take_s(-4, l, 1)

        @pl.when(t == 1)
        def _():
            expand(3, 3, 0, 8)
            expand(1, 3, 0, 8)
            take_s(4, other, 1)
            take(1, 3, 1)
            give(1, 3, 1, sib)
            take(3, 3, 1)
            give(3, 3, 1, sib)

        @pl.when(t == 2)
        def _():
            take(2, 3, 0)
            give(2, 3, 0, sib)
            expand(2, 2, 0, 16)

        @pl.when(t == 3)
        def _():
            densify_at(4)
            expand(1, 3, 8, 8)
            farthest()
            take(1, 2, 0)
            give(1, 2, 0, sib)
            take(3, 2, 0)
            give(3, 2, 0, sib)
            take(2, 3, 1)
            give(2, 3, 1, sib)
            expand(2, 3, 0, 8)
            expand(3, 3, 8, 8)

        return carry

    lax.fori_loop(0, ROWS // TILE, early, 0)

    def late(t):
        here = pl.ds(t * CUT, CUT)
        acc[here, :] += dot(here, ((7, 1), (9, 3), (15, 1)))

    def last(t):
        here = pl.ds(t * CUT, CUT)
        outv[here, :] = (acc[here, :] + dot(here, ((6, 1), (14, 1)))).astype(jnp.bfloat16)
        copy = pltpu.make_async_copy(outv.at[here], out_ref.at[here], in_sem.at[t])
        copy.start()
        return copy

    late(0)
    take(3, 2, 1)
    give(3, 2, 1, sib)
    take(1, 2, 1)
    give(1, 2, 1, sib)
    expand(1, 2, 0, 8)
    expand(3, 2, 0, 8)
    first_half = last(0)
    expand(2, 3, 8, 8)
    late(1)
    expand(3, 2, 8, 8)
    expand(1, 2, 8, 8)
    second_half = last(1)
    first_half.wait()
    second_half.wait()
    for index, ends in enumerate(pending):
        remote(index, ends).wait_send()


def on_device(x_blocks, x_cols, x_scales, x_counts, scale_table, s_panel, s_rows, s_counts):
    hbm = pl.BlockSpec(memory_space=pltpu.HBM)
    return pl.pallas_call(
        kernel,
        out_shape=jax.ShapeDtypeStruct((ROWS, COLS), jnp.bfloat16),
        in_specs=[hbm] * 8,
        out_specs=hbm,
        scratch_shapes=[
            pltpu.VMEM((32, XMSG, 128), jnp.bfloat16),
            pltpu.VMEM((XMSG, 128), jnp.bfloat16),
            pltpu.VMEM((16, SMSG, COLS), jnp.bfloat16),
            pltpu.VMEM((8192, COLS), jnp.bfloat16),
            pltpu.VMEM((ROWS, COLS), jnp.float32),
            pltpu.VMEM((ROWS, 8192), jnp.bfloat16),
            pltpu.VMEM((ROWS, COLS), jnp.bfloat16),
            pltpu.VMEM((32, BLK, 128), jnp.bfloat16),
            pltpu.VMEM((2, 1, 128, COLS), jnp.bfloat16),
            pltpu.SMEM((2, 32), jnp.int32),
            pltpu.SMEM((2, 32), jnp.int32),
            pltpu.SMEM((1, 32), jnp.int32),
            pltpu.SMEM((LEVELS,), jnp.float32),
            pltpu.SMEM((2, 1, 2, 4), jnp.int32),
            pltpu.SMEM((2, 1, 4), jnp.int32),
            pltpu.SemaphoreType.DMA((N_SEND,)),
            pltpu.SemaphoreType.DMA((64,)),
            pltpu.SemaphoreType.DMA((32,)),
            pltpu.SemaphoreType.DMA((8,)),
        ],
        compiler_params=pltpu.CompilerParams(
            collective_id=0, has_side_effects=True, vmem_limit_bytes=60 * 1024 * 1024
        ),
        cost_estimate=pl.CostEstimate(flops=2 * 2048 * 256 * 4096, bytes_accessed=2 << 20, transcendentals=0),
    )(x_blocks, x_cols.T, x_scales.T, x_counts.T, scale_table, s_panel, s_rows, s_counts)


def solution(mesh):
    in_specs = (
        P("row", None, ("col", "layer")),
        P("row", ("col", "layer")),
        P("row", ("col", "layer")),
        P("row", ("col", "layer")),
        P(),
        P("row", "layer", None, "col"),
        P("row", "layer", None, "col"),
        P("row", "layer", "col"),
    )
    out_specs = P(("row", "layer"), "col")
    return jax.shard_map(
        on_device, mesh=mesh, in_specs=in_specs, out_specs=out_specs, check_vma=False
    )
```

```python
import jax
import jax.numpy as jnp
from jax import lax
from jax.experimental import pallas as pl
from jax.experimental.pallas import tpu as pltpu
from jax.sharding import PartitionSpec as P

BLK = 64
KPB = 4
LEVELS = 16
ROWS = 1024
CUT = 512
LIST = 16
XMSG = LIST + ROWS
SROWS = 256
SMSG = SROWS + 16
COLS = 256
TILE = 256
N_SEND = 96
MESH = pl.DeviceIdType.MESH


def kernel(
    x_in, xc_in, xs_in, xn_in, tab_in, s_in, sr_in, sn_in, out_ref,
    xg, xo, sg, sd, acc, xd, outv, x_ref, s_ref, xc_ref, xs_ref, xn_ref, tab_ref, sr_ref, sn_ref,
    send_sem, xsem, ssem, in_sem, plane_sem, column_sem,
):
    z = lax.axis_index("row")
    c = lax.axis_index("col")
    l = lax.axis_index("layer")
    k = c % 2
    x = (c // 2) % 4
    y = (c // 8) * 2 + l
    xr, xl = (x + 1) % 4, (x + 3) % 4
    near = 3 - 2 * l
    yn, yp, yy = (y + near) % 4, (y + 4 - near) % 4, (y + 2) % 4
    ks = 1 - k

    def dev(x_, y_, z_, k_):
        return (z_, (y_ // 2) * 8 + x_ * 2 + k_, y_ % 2)

    def unit(x_, y_):
        return ((y_ // 2) * 4 + x_) * 2 + y_ % 2

    def slot(x_, y_):
        return unit(x_, y_) * 2 + k

    def zat(step):
        return (z + step + 8) % 8

    right, left, sib = dev(xr, y, z, k), dev(xl, y, z, k), dev(x, y, z, ks)
    up, down = dev(x, y, zat(1), k), dev(x, y, zat(-1), k)
    ynear, ypair, yfar = dev(x, yn, z, k), dev(x, yp, z, k), dev(x, yy, z, k)

    barrier = pltpu.get_barrier_semaphore()
    for x_, y_ in ((xr, y), (xl, y), (x, yn), (x, yp), (x, yy)):
        pl.semaphore_signal(barrier, inc=1, device_id=dev(x_, y_, z, 0), device_id_type=MESH)
    for step in (1, -1):
        pl.semaphore_signal(barrier, inc=1, device_id=dev(x, y, zat(step), 1), device_id_type=MESH)
    pl.semaphore_signal(barrier, inc=1, device_id=sib, device_id_type=MESH)

    pending = []

    def remote(index, ends):
        src, dst, recv, target = ends()
        return pltpu.make_async_remote_copy(
            src_ref=src, dst_ref=dst, send_sem=send_sem.at[index], recv_sem=recv,
            device_id=target, device_id_type=MESH,
        )

    def send(ends):
        remote(len(pending), ends).start()
        pending.append(ends)

    def half(ref, h):
        return ref.at[pl.ds(0, LIST + CUT)] if h == 0 else ref.at[pl.ds(LIST + CUT, CUT)]

    def xview(s, h):
        return half(xg.at[s], h)

    def xrecv(s, h):
        pltpu.make_async_remote_copy(
            src_ref=xview(s, h), dst_ref=xview(s, h), send_sem=send_sem.at[0],
            recv_sem=xsem.at[s * 2 + h], device_id=sib, device_id_type=MESH,
        ).wait_recv()

    def sview(u, q):
        return sg.at[u, pl.ds(0, 128)] if q == 0 else sg.at[u, pl.ds(128, SMSG - 128)]

    def srecv(u, q):
        pltpu.make_async_remote_copy(
            src_ref=sview(u, q), dst_ref=sview(u, q), send_sem=send_sem.at[0],
            recv_sem=ssem.at[u * 2 + q], device_id=sib, device_id_type=MESH,
        ).wait_recv()

    copies = [
        pltpu.make_async_copy(src, dst, in_sem.at[i])
        for i, (src, dst) in enumerate((
            (xc_in, xc_ref), (xs_in, xs_ref), (xn_in, xn_ref), (tab_in, tab_ref),
            (sr_in, sr_ref), (sn_in, sn_ref), (x_in, x_ref), (s_in, s_ref),
        ))
    ]
    for copy in copies:
        copy.start()
    for copy in copies:
        copy.wait()

    lane = lax.broadcasted_iota(jnp.int32, (1, 128), 1)
    list_row = lax.broadcasted_iota(jnp.int32, (16, 128), 0)
    list_first = lax.broadcasted_iota(jnp.int32, (16, 128), 1) < BLK

    def fill(dst, which):
        def row(i, cols):
            for i4 in range(4):
                r = i * 4 + i4
                at = which * 16 + r
                count = xn_ref[0, at]
                f0 = jnp.where(count > 0, tab_ref[xs_ref[0, at]], 0.0)
                f1 = jnp.where(count > 1, tab_ref[xs_ref[1, at]], 0.0)
                scaled = x_ref[at].astype(jnp.float32) * jnp.where(lane < BLK, f0, f1)
                dst[pl.ds(pl.multiple_of(LIST + r * BLK, LIST), BLK), :] = scaled.astype(jnp.bfloat16)
                cols = jnp.where(list_row == r, jnp.where(list_first, xc_ref[0, at], xc_ref[1, at]), cols)
            return cols

        cols = lax.fori_loop(0, 4, row, jnp.zeros((16, 128), jnp.int32))
        dst[pl.ds(0, LIST), :] = cols.astype(jnp.float32).astype(jnp.bfloat16)

    own = slot(x, y)
    fill(xg.at[own], l)
    fill(xo, 1 - l)

    own_s = z * 2 + l
    other = 1 - l
    s_block = lax.broadcasted_iota(jnp.int32, (16, COLS), 1) // BLK
    s_row = lax.broadcasted_iota(jnp.int32, (16, COLS), 0)
    rows = jnp.full((16, COLS), KPB, jnp.int32)
    for j in range(2):
        for b in range(COLS // BLK):
            for w in range(2):
                live_row = jnp.where(w < sn_ref[j, 0, b], sr_ref[j, 0, w, b], KPB)
                rows = jnp.where((s_block == b) & (s_row == 2 * j + w), live_row, rows)
    sg[own_s, pl.ds(0, 128), :] = s_ref[0, 0]
    sg[own_s, pl.ds(128, 128), :] = s_ref[1, 0]
    sg[own_s, pl.ds(SROWS, 16), :] = rows.astype(jnp.float32).astype(jnp.bfloat16)

    def s_at(step, layer):
        return zat(step) * 2 + layer

    def at(e, m):
        return slot((x + e) % 4, (y + along_y(m)) % 4)

    def take(e, m, h):
        xrecv(at(e, m), h)

    def give(e, m, h, target):
        def ends():
            s = at(e, m)
            return xview(s, h), xview(s, h), xsem.at[s * 2 + h], target

        send(ends)

    def take_s(step, layer, q):
        srecv(s_at(step, layer), q)

    def give_s(step, layer, q, target):
        def ends():
            u = s_at(step, layer)
            return sview(u, q), sview(u, q), ssem.at[u * 2 + q], target

        send(ends)

    lane_half = lax.broadcasted_iota(jnp.int32, (LIST, 128), 1) // BLK

    def along_y(m):
        return (m * near) % 4

    def expand(e, m, start, count):
        u = unit((x + e) % 4, (y + along_y(m)) % 4)
        first = (e * 4 + m) * 512
        for h in range(start // 8, (start + count) // 8):
            xrecv(u * 2 + ks, h)
        for j in range(2):
            code = xg[u * 2 + j, pl.ds(0, LIST), :].astype(jnp.float32)
            turned_code = pltpu.roll(code, BLK, 1)
            kept, moved = [], []
            for q in range(2):
                want = (lane_half + 2 * q).astype(jnp.float32)
                kept.append(jnp.where(code == want, 1.0, 0.0).astype(jnp.bfloat16))
                moved.append(jnp.where(turned_code == want, 1.0, 0.0).astype(jnp.bfloat16))
            for r in range(start, start + count):
                block = xg[u * 2 + j, pl.ds(LIST + r * BLK, BLK), :]
                turned = pltpu.roll(block, BLK, 1)
                for q in range(2):
                    xd[pl.ds(r * BLK, BLK), pl.ds(first + j * 256 + q * 128, 128)] = (
                        block * kept[q][r : r + 1] + turned * moved[q][r : r + 1]
                    )

    def place(u):
        return ((u // 2) % 4 - x + 4) % 4, (((u // 8) * 2 + u % 2 - y + 4) * near) % 4

    def densify(u):
        e, m = place(u)
        first = (e * 4 + m) * 512
        for j in range(2):
            r0 = sg[u, pl.ds(SROWS, 16), :].astype(jnp.float32)
            for kb in range(KPB):
                m0 = jnp.where(r0[2 * j : 2 * j + 1] == kb, 1.0, 0.0).astype(jnp.bfloat16)
                m1 = jnp.where(r0[2 * j + 1 : 2 * j + 2] == kb, 1.0, 0.0).astype(jnp.bfloat16)
                sd[pl.ds(pl.multiple_of(first + j * 256 + kb * BLK, BLK), BLK), :] = (
                    sg[u, pl.ds(j * 128, BLK), :] * m0 + sg[u, pl.ds(j * 128 + BLK, BLK), :] * m1
                )

    def densify_at(distance):
        def one(i, carry):
            densify(s_at((2 * (i // 2) - 1) * distance, i % 2))
            return carry

        lax.fori_loop(0, 2 if distance in (0, 4) else 4, one, 0)

    def dot(here, ranges):
        total = None
        for first, count in ranges:
            k = pl.ds(first * 512, count * 512)
            term = jnp.dot(xd[here, k], sd[k, :], preferred_element_type=jnp.float32)
            total = term if total is None else total + term
        return total

    @pl.when(k == 0)
    def _():
        pl.semaphore_wait(barrier, 11)
        pl.semaphore_signal(plane_sem, inc=1, device_id=sib, device_id_type=MESH)

    @pl.when(k == 1)
    def _():
        pl.semaphore_wait(plane_sem, 1)


    give(0, 0, 0, right)
    give(0, 0, 1, left)
    for q in range(2):
        give_s(0, l, q, ypair)
    give(0, 0, 1, right)
    give(0, 0, 0, left)
    for h in range(2):
        for target in (ynear, ypair):
            send(lambda h=h, target=target: (half(xo, h), xview(own, h), xsem.at[own * 2 + h], target))
    for h in range(2):
        give(0, 0, h, sib)
    for h in range(2):
        give(0, 0, h, yfar)

    @pl.when(k == 1)
    def _():
        pl.semaphore_wait(barrier, 5)
        pl.semaphore_signal(column_sem, inc=1, device_id=sib, device_id_type=MESH)

    @pl.when(k == 0)
    def _():
        pl.semaphore_wait(column_sem, 1)

    for q in range(2):
        give_s(0, l, q, up)
        give_s(0, l, q, down)

    def clear(i, carry):
        e, m = place(s_at(4, i))
        sd[pl.ds(pl.multiple_of((e * 4 + m) * 512, 512), 512), :] = jnp.zeros((512, COLS), jnp.bfloat16)
        return carry

    lax.fori_loop(0, 2, clear, 0)
    sd[pl.ds(8192, 512), :] = jnp.zeros((512, COLS), jnp.bfloat16)

    expand(0, 0, 0, 16)
    take_s(0, other, 0)
    give_s(0, other, 0, up)
    give_s(0, other, 0, down)
    take(3, 0, 0)
    give(3, 0, 0, right)
    give(3, 0, 0, sib)
    take_s(0, other, 1)
    give_s(0, other, 1, up)
    give_s(0, other, 1, down)
    densify_at(0)
    take(0, 1, 0)
    give(0, 1, 0, right)
    give(0, 1, 0, left)
    give(0, 1, 0, sib)
    take_s(-1, l, 0)
    give_s(-1, l, 0, up)
    take_s(1, l, 0)
    give_s(1, l, 0, down)
    take(3, 0, 1)
    give(3, 0, 1, sib)
    take_s(-1, l, 1)
    give_s(-1, l, 1, up)
    take(1, 0, 0)
    give(1, 0, 0, sib)
    take_s(1, l, 1)
    give_s(1, l, 1, down)
    take(0, 1, 1)
    give(0, 1, 1, left)
    take(1, 0, 1)
    give(1, 0, 1, left)
    give(0, 1, 1, right)
    give(1, 0, 1, sib)
    give(0, 1, 1, sib)
    take_s(-1, other, 0)
    give_s(-1, other, 0, up)
    take_s(1, other, 0)
    give_s(1, other, 0, down)
    expand(3, 0, 0, 16)
    take(2, 0, 0)
    give(2, 0, 0, yfar)
    give(2, 0, 0, sib)
    take_s(-1, other, 1)
    give_s(-1, other, 1, up)
    take(1, 1, 0)
    give(1, 1, 0, sib)
    take_s(1, other, 1)
    give_s(1, other, 1, down)
    expand(1, 0, 0, 16)
    take_s(-2, l, 0)
    give_s(-2, l, 0, up)
    take_s(2, l, 0)
    give_s(2, l, 0, down)
    expand(0, 1, 0, 16)
    densify_at(1)
    take_s(-2, l, 1)
    give_s(-2, l, 1, up)
    take_s(2, l, 1)
    give_s(2, l, 1, down)
    take(3, 1, 0)
    give(3, 1, 0, right)
    take(1, 1, 1)
    give(1, 1, 1, left)
    take(0, 3, 0)
    give(0, 3, 0, right)
    give(0, 3, 0, left)
    take(0, 3, 1)
    give(0, 3, 1, right)
    give(0, 3, 1, left)
    take(0, 2, 0)
    give(0, 2, 0, right)
    give(0, 2, 0, left)
    give(3, 1, 0, sib)
    take_s(-2, other, 0)
    give_s(-2, other, 0, up)
    take_s(2, other, 0)
    give_s(2, other, 0, down)
    give(1, 1, 1, sib)
    give(0, 3, 0, sib)
    take(0, 2, 1)
    give(0, 2, 1, right)
    give(0, 2, 1, left)
    give(0, 3, 1, sib)
    give(0, 2, 0, sib)
    give(0, 2, 1, sib)
    take_s(-2, other, 1)
    give_s(-2, other, 1, up)
    take_s(2, other, 1)
    give_s(2, other, 1, down)
    densify_at(2)
    take(3, 1, 1)
    give(3, 1, 1, sib)
    take(2, 0, 1)
    give(2, 0, 1, yfar)
    give(2, 0, 1, sib)
    expand(1, 1, 0, 16)
    take_s(-3, l, 0)
    give_s(-3, l, 0, up)
    take_s(3, l, 0)
    take(2, 2, 0)
    give(2, 2, 0, sib)
    expand(0, 3, 0, 16)
    expand(0, 2, 0, 16)
    take_s(-3, l, 1)
    give_s(-3, l, 1, up)
    expand(3, 1, 0, 16)
    take_s(3, l, 1)
    take(2, 1, 1)
    give(2, 1, 1, yfar)
    take(2, 1, 0)
    give(2, 1, 0, yfar)
    give(2, 1, 0, sib)
    give(2, 1, 1, sib)
    expand(2, 0, 0, 16)
    take_s(-3, other, 0)
    take_s(3, other, 0)
    give_s(3, other, 0, down)
    take_s(-3, other, 1)
    take_s(3, other, 1)
    give_s(3, other, 1, down)
    densify_at(3)
    take(1, 3, 0)
    give(1, 3, 0, sib)
    take(3, 3, 0)
    give(3, 3, 0, sib)
    take(2, 2, 1)
    give(2, 2, 1, sib)
    expand(2, 1, 0, 16)

    def early(t, carry):
        here = pl.ds(pl.multiple_of(t * TILE, TILE), TILE)
        acc[here, :] = dot(here, ((0, 4), (4, 2), (8, 1), (12, 2)))

        @pl.when(t == 2)
        def _():
            take(1, 3, 1)
            give(1, 3, 1, sib)
            take(3, 3, 1)
            give(3, 3, 1, sib)
            take(2, 3, 1)
            give(2, 3, 1, sib)
            expand(1, 3, 0, 8)
            expand(2, 2, 0, 16)
            expand(3, 3, 0, 8)

        @pl.when(t == 3)
        def _():
            expand(1, 3, 8, 8)
            take(1, 2, 0)
            give(1, 2, 0, sib)
            expand(3, 3, 8, 8)
            take(3, 2, 0)
            give(3, 2, 0, sib)
            take(2, 3, 0)
            give(2, 3, 0, sib)
            expand(1, 2, 0, 8)
            expand(3, 2, 0, 8)
            take(1, 2, 1)
            give(1, 2, 1, sib)
            take(3, 2, 1)
            give(3, 2, 1, sib)
            expand(2, 3, 0, 8)
            expand(2, 3, 8, 8)

        return carry

    lax.fori_loop(0, ROWS // TILE, early, 0)

    def late(t):
        here = pl.ds(t * CUT, CUT)
        acc[here, :] += dot(here, ((7, 1), (9, 3), (15, 1)))

    def last(t):
        here = pl.ds(t * CUT, CUT)
        total = acc[here, :] + dot(here, ((6, 1), (14, 1)))
        for i in range(2):
            e, m = place(s_at(4, i))
            first = (e * 4 + m) * 512
            counted = (e % 2) * (m // 2) * (1 - m % 2)
            k_x = pl.ds(pl.multiple_of(first, 512), 512)
            k_s = pl.ds(pl.multiple_of(first + counted * (8192 - first), 512), 512)
            total += jnp.dot(xd[here, k_x], sd[k_s, :], preferred_element_type=jnp.float32)
        outv[here, :] = total.astype(jnp.bfloat16)
        copy = pltpu.make_async_copy(outv.at[here], out_ref.at[here], in_sem.at[t])
        copy.start()
        return copy

    late(0)

    late(1)
    take_s(-4, l, 0)
    take_s(4, other, 0)
    take_s(-4, l, 1)
    take_s(4, other, 1)
    expand(1, 2, 8, 8)
    densify_at(4)
    expand(3, 2, 8, 8)
    first_half = last(0)

    second_half = last(1)
    first_half.wait()
    second_half.wait()
    for index, ends in enumerate(pending):
        remote(index, ends).wait_send()


def on_device(x_blocks, x_cols, x_scales, x_counts, scale_table, s_panel, s_rows, s_counts):
    hbm = pl.BlockSpec(memory_space=pltpu.HBM)
    return pl.pallas_call(
        kernel,
        out_shape=jax.ShapeDtypeStruct((ROWS, COLS), jnp.bfloat16),
        in_specs=[hbm] * 8,
        out_specs=hbm,
        scratch_shapes=[
            pltpu.VMEM((32, XMSG, 128), jnp.bfloat16),
            pltpu.VMEM((XMSG, 128), jnp.bfloat16),
            pltpu.VMEM((16, SMSG, COLS), jnp.bfloat16),
            pltpu.VMEM((8192 + 512, COLS), jnp.bfloat16),
            pltpu.VMEM((ROWS, COLS), jnp.float32),
            pltpu.VMEM((ROWS, 8192), jnp.bfloat16),
            pltpu.VMEM((ROWS, COLS), jnp.bfloat16),
            pltpu.VMEM((32, BLK, 128), jnp.bfloat16),
            pltpu.VMEM((2, 1, 128, COLS), jnp.bfloat16),
            pltpu.SMEM((2, 32), jnp.int32),
            pltpu.SMEM((2, 32), jnp.int32),
            pltpu.SMEM((1, 32), jnp.int32),
            pltpu.SMEM((LEVELS,), jnp.float32),
            pltpu.SMEM((2, 1, 2, 4), jnp.int32),
            pltpu.SMEM((2, 1, 4), jnp.int32),
            pltpu.SemaphoreType.DMA((N_SEND,)),
            pltpu.SemaphoreType.DMA((64,)),
            pltpu.SemaphoreType.DMA((32,)),
            pltpu.SemaphoreType.DMA((8,)),
            pltpu.SemaphoreType.REGULAR,
            pltpu.SemaphoreType.REGULAR,
        ],
        compiler_params=pltpu.CompilerParams(
            collective_id=0, has_side_effects=True, vmem_limit_bytes=60 * 1024 * 1024
        ),
        cost_estimate=pl.CostEstimate(flops=2 * 2048 * 256 * 4096, bytes_accessed=2 << 20, transcendentals=0),
    )(x_blocks, x_cols.T, x_scales.T, x_counts.T, scale_table, s_panel, s_rows, s_counts)


def solution(mesh):
    in_specs = (
        P("row", None, ("col", "layer")),
        P("row", ("col", "layer")),
        P("row", ("col", "layer")),
        P("row", ("col", "layer")),
        P(),
        P("row", "layer", None, "col"),
        P("row", "layer", None, "col"),
        P("row", "layer", "col"),
    )
    out_specs = P(("row", "layer"), "col")
    return jax.shard_map(
        on_device, mesh=mesh, in_specs=in_specs, out_specs=out_specs, check_vma=False
    )
```

```python
import jax
import jax.numpy as jnp
from jax import lax
from jax.experimental import pallas as pl
from jax.experimental.pallas import tpu as pltpu
from jax.sharding import PartitionSpec as P

BLK = 64
KPB = 4
LEVELS = 16
ROWS = 1024
CUT = 512
LIST = 16
XMSG = LIST + ROWS
SROWS = 256
SMSG = SROWS + 16
COLS = 256
TILE = 256
N_SEND = 96
MESH = pl.DeviceIdType.MESH


def kernel(
    x_in, xc_in, xs_in, xn_in, tab_in, s_in, sr_in, sn_in, out_ref,
    xg, xo, sg, sd, acc, xd, outv, x_ref, s_ref, xc_ref, xs_ref, xn_ref, tab_ref, sr_ref, sn_ref,
    send_sem, xsem, ssem, in_sem, plane_sem, column_sem,
):
    z = lax.axis_index("row")
    c = lax.axis_index("col")
    l = lax.axis_index("layer")
    k = c % 2
    x = (c // 2) % 4
    y = (c // 8) * 2 + l
    xr, xl = (x + 1) % 4, (x + 3) % 4
    near = 3 - 2 * l
    yn, yp, yy = (y + near) % 4, (y + 4 - near) % 4, (y + 2) % 4
    ks = 1 - k

    def dev(x_, y_, z_, k_):
        return (z_, (y_ // 2) * 8 + x_ * 2 + k_, y_ % 2)

    def unit(x_, y_):
        return ((y_ // 2) * 4 + x_) * 2 + y_ % 2

    def slot(x_, y_):
        return unit(x_, y_) * 2 + k

    def zat(step):
        return (z + step + 8) % 8

    right, left, sib = dev(xr, y, z, k), dev(xl, y, z, k), dev(x, y, z, ks)
    up, down = dev(x, y, zat(1), k), dev(x, y, zat(-1), k)
    ynear, ypair, yfar = dev(x, yn, z, k), dev(x, yp, z, k), dev(x, yy, z, k)

    barrier = pltpu.get_barrier_semaphore()
    for x_, y_ in ((xr, y), (xl, y), (x, yn), (x, yp), (x, yy)):
        pl.semaphore_signal(barrier, inc=1, device_id=dev(x_, y_, z, 0), device_id_type=MESH)
    for step in (1, -1):
        pl.semaphore_signal(barrier, inc=1, device_id=dev(x, y, zat(step), 1), device_id_type=MESH)
    pl.semaphore_signal(barrier, inc=1, device_id=sib, device_id_type=MESH)

    pending = []

    def remote(index, ends):
        src, dst, recv, target = ends()
        return pltpu.make_async_remote_copy(
            src_ref=src, dst_ref=dst, send_sem=send_sem.at[index], recv_sem=recv,
            device_id=target, device_id_type=MESH,
        )

    def send(ends):
        remote(len(pending), ends).start()
        pending.append(ends)

    def half(ref, h):
        return ref.at[pl.ds(0, LIST + CUT)] if h == 0 else ref.at[pl.ds(LIST + CUT, CUT)]

    def xview(s, h):
        return half(xg.at[s], h)

    def xrecv(s, h):
        pltpu.make_async_remote_copy(
            src_ref=xview(s, h), dst_ref=xview(s, h), send_sem=send_sem.at[0],
            recv_sem=xsem.at[s * 2 + h], device_id=sib, device_id_type=MESH,
        ).wait_recv()

    def sview(u, q):
        return sg.at[u, pl.ds(0, 128)] if q == 0 else sg.at[u, pl.ds(128, SMSG - 128)]

    def srecv(u, q):
        pltpu.make_async_remote_copy(
            src_ref=sview(u, q), dst_ref=sview(u, q), send_sem=send_sem.at[0],
            recv_sem=ssem.at[u * 2 + q], device_id=sib, device_id_type=MESH,
        ).wait_recv()

    copies = [
        pltpu.make_async_copy(src, dst, in_sem.at[i])
        for i, (src, dst) in enumerate((
            (xc_in, xc_ref), (xs_in, xs_ref), (xn_in, xn_ref), (tab_in, tab_ref),
            (sr_in, sr_ref), (sn_in, sn_ref), (x_in, x_ref), (s_in, s_ref),
        ))
    ]
    for copy in copies:
        copy.start()
    for copy in copies:
        copy.wait()

    lane = lax.broadcasted_iota(jnp.int32, (1, 128), 1)
    list_row = lax.broadcasted_iota(jnp.int32, (16, 128), 0)
    list_first = lax.broadcasted_iota(jnp.int32, (16, 128), 1) < BLK

    def fill(dst, which):
        def row(i, cols):
            for i4 in range(4):
                r = i * 4 + i4
                at = which * 16 + r
                count = xn_ref[0, at]
                f0 = jnp.where(count > 0, tab_ref[xs_ref[0, at]], 0.0)
                f1 = jnp.where(count > 1, tab_ref[xs_ref[1, at]], 0.0)
                scaled = x_ref[at].astype(jnp.float32) * jnp.where(lane < BLK, f0, f1)
                dst[pl.ds(pl.multiple_of(LIST + r * BLK, LIST), BLK), :] = scaled.astype(jnp.bfloat16)
                cols = jnp.where(list_row == r, jnp.where(list_first, xc_ref[0, at], xc_ref[1, at]), cols)
            return cols

        cols = lax.fori_loop(0, 4, row, jnp.zeros((16, 128), jnp.int32))
        dst[pl.ds(0, LIST), :] = cols.astype(jnp.float32).astype(jnp.bfloat16)

    own = slot(x, y)
    fill(xg.at[own], l)
    fill(xo, 1 - l)

    own_s = z * 2 + l
    other = 1 - l
    s_block = lax.broadcasted_iota(jnp.int32, (16, COLS), 1) // BLK
    s_row = lax.broadcasted_iota(jnp.int32, (16, COLS), 0)
    rows = jnp.full((16, COLS), KPB, jnp.int32)
    for j in range(2):
        for b in range(COLS // BLK):
            for w in range(2):
                live_row = jnp.where(w < sn_ref[j, 0, b], sr_ref[j, 0, w, b], KPB)
                rows = jnp.where((s_block == b) & (s_row == 2 * j + w), live_row, rows)
    sg[own_s, pl.ds(0, 128), :] = s_ref[0, 0]
    sg[own_s, pl.ds(128, 128), :] = s_ref[1, 0]
    sg[own_s, pl.ds(SROWS, 16), :] = rows.astype(jnp.float32).astype(jnp.bfloat16)

    def s_at(step, layer):
        return zat(step) * 2 + layer

    def at(e, m):
        return slot((x + e) % 4, (y + along_y(m)) % 4)

    def take(e, m, h):
        xrecv(at(e, m), h)

    def give(e, m, h, target):
        def ends():
            s = at(e, m)
            return xview(s, h), xview(s, h), xsem.at[s * 2 + h], target

        send(ends)

    def take_s(step, layer, q):
        srecv(s_at(step, layer), q)

    def give_s(step, layer, q, target):
        def ends():
            u = s_at(step, layer)
            return sview(u, q), sview(u, q), ssem.at[u * 2 + q], target

        send(ends)

    lane_half = lax.broadcasted_iota(jnp.int32, (LIST, 128), 1) // BLK

    def along_y(m):
        return (m * near) % 4

    def expand(e, m, start, count):
        u = unit((x + e) % 4, (y + along_y(m)) % 4)
        first = (e * 4 + m) * 512
        for h in range(start // 8, (start + count) // 8):
            xrecv(u * 2 + ks, h)
        for j in range(2):
            code = xg[u * 2 + j, pl.ds(0, LIST), :].astype(jnp.float32)
            turned_code = pltpu.roll(code, BLK, 1)
            kept, moved = [], []
            for q in range(2):
                want = (lane_half + 2 * q).astype(jnp.float32)
                kept.append(jnp.where(code == want, 1.0, 0.0).astype(jnp.bfloat16))
                moved.append(jnp.where(turned_code == want, 1.0, 0.0).astype(jnp.bfloat16))
            for r in range(start, start + count):
                block = xg[u * 2 + j, pl.ds(LIST + r * BLK, BLK), :]
                turned = pltpu.roll(block, BLK, 1)
                for q in range(2):
                    xd[pl.ds(r * BLK, BLK), pl.ds(first + j * 256 + q * 128, 128)] = (
                        block * kept[q][r : r + 1] + turned * moved[q][r : r + 1]
                    )

    def place(u):
        return ((u // 2) % 4 - x + 4) % 4, (((u // 8) * 2 + u % 2 - y + 4) * near) % 4

    def densify(u):
        e, m = place(u)
        first = (e * 4 + m) * 512
        for j in range(2):
            r0 = sg[u, pl.ds(SROWS, 16), :].astype(jnp.float32)
            for kb in range(KPB):
                m0 = jnp.where(r0[2 * j : 2 * j + 1] == kb, 1.0, 0.0).astype(jnp.bfloat16)
                m1 = jnp.where(r0[2 * j + 1 : 2 * j + 2] == kb, 1.0, 0.0).astype(jnp.bfloat16)
                sd[pl.ds(pl.multiple_of(first + j * 256 + kb * BLK, BLK), BLK), :] = (
                    sg[u, pl.ds(j * 128, BLK), :] * m0 + sg[u, pl.ds(j * 128 + BLK, BLK), :] * m1
                )

    def densify_at(distance):
        def one(i, carry):
            densify(s_at((2 * (i // 2) - 1) * distance, i % 2))
            return carry

        lax.fori_loop(0, 2 if distance in (0, 4) else 4, one, 0)

    def dot(here, ranges):
        total = None
        for first, count in ranges:
            k = pl.ds(first * 512, count * 512)
            term = jnp.dot(xd[here, k], sd[k, :], preferred_element_type=jnp.float32)
            total = term if total is None else total + term
        return total

    @pl.when(k == 0)
    def _():
        pl.semaphore_wait(barrier, 11)
        pl.semaphore_signal(plane_sem, inc=1, device_id=sib, device_id_type=MESH)

    @pl.when(k == 1)
    def _():
        pl.semaphore_wait(plane_sem, 1)


    give(0, 0, 0, right)
    give(0, 0, 1, left)
    for q in range(2):
        give_s(0, l, q, ypair)
    give(0, 0, 1, right)
    give(0, 0, 0, left)
    for h in range(2):
        for target in (ynear, ypair):
            send(lambda h=h, target=target: (half(xo, h), xview(own, h), xsem.at[own * 2 + h], target))
    for h in range(2):
        give(0, 0, h, sib)
    for h in range(2):
        give(0, 0, h, yfar)

    @pl.when(k == 1)
    def _():
        pl.semaphore_wait(barrier, 5)
        pl.semaphore_signal(column_sem, inc=1, device_id=sib, device_id_type=MESH)

    @pl.when(k == 0)
    def _():
        pl.semaphore_wait(column_sem, 1)

    for q in range(2):
        give_s(0, l, q, up)
        give_s(0, l, q, down)

    def clear(i, carry):
        e, m = place(s_at(4, i))
        sd[pl.ds(pl.multiple_of((e * 4 + m) * 512, 512), 512), :] = jnp.zeros((512, COLS), jnp.bfloat16)
        return carry

    lax.fori_loop(0, 2, clear, 0)
    sd[pl.ds(8192, 512), :] = jnp.zeros((512, COLS), jnp.bfloat16)

    expand(0, 0, 0, 16)
    take_s(0, other, 0)
    give_s(0, other, 0, up)
    give_s(0, other, 0, down)
    take(3, 0, 0)
    give(3, 0, 0, right)
    give(3, 0, 0, sib)
    take_s(0, other, 1)
    give_s(0, other, 1, up)
    give_s(0, other, 1, down)
    densify_at(0)
    take(0, 1, 0)
    give(0, 1, 0, left)
    give(0, 1, 0, right)
    give(0, 1, 0, sib)
    take_s(-1, l, 0)
    give_s(-1, l, 0, up)
    take_s(1, l, 0)
    give_s(1, l, 0, down)
    take(3, 0, 1)
    give(3, 0, 1, sib)
    take(1, 0, 0)
    give(1, 0, 0, sib)
    take_s(-1, l, 1)
    give_s(-1, l, 1, up)
    take(0, 1, 1)
    give(0, 1, 1, right)
    take_s(1, l, 1)
    give_s(1, l, 1, down)
    give(0, 1, 1, left)
    take(1, 0, 1)
    give(1, 0, 1, left)
    give(1, 0, 1, sib)
    give(0, 1, 1, sib)
    take_s(-1, other, 0)
    give_s(-1, other, 0, up)
    take_s(1, other, 0)
    give_s(1, other, 0, down)
    expand(3, 0, 0, 16)
    take(2, 0, 0)
    give(2, 0, 0, yfar)
    give(2, 0, 0, sib)
    take(1, 1, 0)
    give(1, 1, 0, sib)
    expand(1, 0, 0, 16)
    take_s(-1, other, 1)
    give_s(-1, other, 1, up)
    take_s(1, other, 1)
    give_s(1, other, 1, down)
    expand(0, 1, 0, 16)
    take_s(-2, l, 0)
    give_s(-2, l, 0, up)
    take_s(2, l, 0)
    give_s(2, l, 0, down)
    densify_at(1)
    take_s(-2, l, 1)
    give_s(-2, l, 1, up)
    take_s(2, l, 1)
    give_s(2, l, 1, down)
    take(3, 1, 0)
    give(3, 1, 0, right)
    give(3, 1, 0, sib)
    take(1, 1, 1)
    give(1, 1, 1, left)
    take(0, 3, 0)
    give(0, 3, 0, right)
    give(0, 3, 0, left)
    take(0, 3, 1)
    give(0, 3, 1, right)
    give(0, 3, 1, left)
    take(0, 2, 0)
    give(0, 2, 0, right)
    give(0, 2, 0, left)
    give(1, 1, 1, sib)
    take_s(-2, other, 0)
    give_s(-2, other, 0, up)
    take(0, 2, 1)
    give(0, 2, 1, right)
    take_s(2, other, 0)
    give_s(2, other, 0, down)
    give(0, 2, 1, left)
    give(0, 3, 0, sib)
    give(0, 3, 1, sib)
    give(0, 2, 0, sib)
    give(0, 2, 1, sib)
    take_s(-2, other, 1)
    give_s(-2, other, 1, up)
    take_s(2, other, 1)
    give_s(2, other, 1, down)
    take(3, 1, 1)
    give(3, 1, 1, sib)
    densify_at(2)
    take(2, 0, 1)
    give(2, 0, 1, yfar)
    give(2, 0, 1, sib)
    expand(1, 1, 0, 16)
    take_s(-3, l, 0)
    give_s(-3, l, 0, up)
    take(2, 2, 0)
    give(2, 2, 0, sib)
    take_s(3, l, 0)
    expand(0, 3, 0, 16)
    expand(0, 2, 0, 16)
    expand(3, 1, 0, 16)
    take_s(-3, l, 1)
    give_s(-3, l, 1, up)
    take_s(3, l, 1)
    take(2, 1, 0)
    give(2, 1, 0, yfar)
    take(2, 1, 1)
    give(2, 1, 1, yfar)
    give(2, 1, 0, sib)
    give(2, 1, 1, sib)
    expand(2, 0, 0, 16)
    take_s(-3, other, 0)
    take_s(3, other, 0)
    give_s(3, other, 0, down)
    take(3, 3, 0)
    give(3, 3, 0, sib)
    take_s(-3, other, 1)
    take(1, 3, 0)
    give(1, 3, 0, sib)
    take_s(3, other, 1)
    give_s(3, other, 1, down)
    expand(2, 1, 0, 16)
    take(2, 2, 1)
    give(2, 2, 1, sib)
    densify_at(3)

    def early(t, carry):
        here = pl.ds(pl.multiple_of(t * TILE, TILE), TILE)
        acc[here, :] = dot(here, ((0, 4), (4, 2), (8, 1), (12, 2)))

        @pl.when(t == 1)
        def _():
            expand(3, 3, 0, 8)
            take(3, 3, 1)
            give(3, 3, 1, sib)
            expand(1, 3, 0, 8)
            take(1, 3, 1)
            give(1, 3, 1, sib)
            expand(2, 2, 0, 16)
            take(2, 3, 0)
            give(2, 3, 0, sib)

        @pl.when(t == 3)
        def _():
            expand(3, 3, 8, 8)
            expand(1, 3, 8, 8)
            take(3, 2, 0)
            give(3, 2, 0, sib)
            take(1, 2, 0)
            give(1, 2, 0, sib)
            expand(2, 3, 0, 8)

        return carry

    lax.fori_loop(0, ROWS // TILE, early, 0)

    def late(t):
        here = pl.ds(t * CUT, CUT)
        acc[here, :] += dot(here, ((7, 1), (9, 3), (15, 1)))

    def last(t):
        here = pl.ds(t * CUT, CUT)
        total = acc[here, :] + dot(here, ((6, 1), (14, 1)))
        for i in range(2):
            e, m = place(s_at(4, i))
            first = (e * 4 + m) * 512
            counted = (e % 2) * (m // 2) * (1 - m % 2)
            k_x = pl.ds(pl.multiple_of(first, 512), 512)
            k_s = pl.ds(pl.multiple_of(first + counted * (8192 - first), 512), 512)
            total += jnp.dot(xd[here, k_x], sd[k_s, :], preferred_element_type=jnp.float32)
        outv[here, :] = total.astype(jnp.bfloat16)
        copy = pltpu.make_async_copy(outv.at[here], out_ref.at[here], in_sem.at[t])
        copy.start()
        return copy

    late(0)
    take(2, 3, 1)
    give(2, 3, 1, sib)
    expand(3, 2, 0, 8)
    expand(1, 2, 0, 8)
    take(3, 2, 1)
    give(3, 2, 1, sib)
    take(1, 2, 1)
    give(1, 2, 1, sib)
    expand(2, 3, 8, 8)
    late(1)
    take_s(-4, l, 0)
    take_s(4, other, 0)
    take_s(-4, l, 1)
    take_s(4, other, 1)
    densify_at(4)
    first_half = last(0)
    expand(1, 2, 8, 8)
    expand(3, 2, 8, 8)
    second_half = last(1)
    first_half.wait()
    second_half.wait()
    for index, ends in enumerate(pending):
        remote(index, ends).wait_send()


def on_device(x_blocks, x_cols, x_scales, x_counts, scale_table, s_panel, s_rows, s_counts):
    hbm = pl.BlockSpec(memory_space=pltpu.HBM)
    return pl.pallas_call(
        kernel,
        out_shape=jax.ShapeDtypeStruct((ROWS, COLS), jnp.bfloat16),
        in_specs=[hbm] * 8,
        out_specs=hbm,
        scratch_shapes=[
            pltpu.VMEM((32, XMSG, 128), jnp.bfloat16),
            pltpu.VMEM((XMSG, 128), jnp.bfloat16),
            pltpu.VMEM((16, SMSG, COLS), jnp.bfloat16),
            pltpu.VMEM((8192 + 512, COLS), jnp.bfloat16),
            pltpu.VMEM((ROWS, COLS), jnp.float32),
            pltpu.VMEM((ROWS, 8192), jnp.bfloat16),
            pltpu.VMEM((ROWS, COLS), jnp.bfloat16),
            pltpu.VMEM((32, BLK, 128), jnp.bfloat16),
            pltpu.VMEM((2, 1, 128, COLS), jnp.bfloat16),
            pltpu.SMEM((2, 32), jnp.int32),
            pltpu.SMEM((2, 32), jnp.int32),
            pltpu.SMEM((1, 32), jnp.int32),
            pltpu.SMEM((LEVELS,), jnp.float32),
            pltpu.SMEM((2, 1, 2, 4), jnp.int32),
            pltpu.SMEM((2, 1, 4), jnp.int32),
            pltpu.SemaphoreType.DMA((N_SEND,)),
            pltpu.SemaphoreType.DMA((64,)),
            pltpu.SemaphoreType.DMA((32,)),
            pltpu.SemaphoreType.DMA((8,)),
            pltpu.SemaphoreType.REGULAR,
            pltpu.SemaphoreType.REGULAR,
        ],
        compiler_params=pltpu.CompilerParams(
            collective_id=0, has_side_effects=True, vmem_limit_bytes=60 * 1024 * 1024
        ),
        cost_estimate=pl.CostEstimate(flops=2 * 2048 * 256 * 4096, bytes_accessed=2 << 20, transcendentals=0),
    )(x_blocks, x_cols.T, x_scales.T, x_counts.T, scale_table, s_panel, s_rows, s_counts)


def solution(mesh):
    in_specs = (
        P("row", None, ("col", "layer")),
        P("row", ("col", "layer")),
        P("row", ("col", "layer")),
        P("row", ("col", "layer")),
        P(),
        P("row", "layer", None, "col"),
        P("row", "layer", None, "col"),
        P("row", "layer", "col"),
    )
    out_specs = P(("row", "layer"), "col")
    return jax.shard_map(
        on_device, mesh=mesh, in_specs=in_specs, out_specs=out_specs, check_vma=False
    )
```
